512 devices in a mesh: dp: 16 (over z), ctx: 32 (over y, x, core).
Axes of the slice: x: 4, y: 4, z: 16, core: 2. Of those that a mesh axis runs over, the one named last changes fastest.
Arguments:
- query_matrix: bfloat16 [65536, 1280], P(('dp', 'ctx')), parts along dimension 0, may hold values from -6 to 6
- address_matrix: bfloat16 [65536, 1280], P(('dp', 'ctx')), parts along dimension 0, may hold values from -6 to 6
- content_matrix: bfloat16 [65536, 1280], P(('dp', 'ctx')), parts along dimension 0, may hold values from -24 to 24
- erasure_vector_raw: bfloat16 [65536, 1280], P(('dp', 'ctx')), parts along dimension 0, may hold values from -16 to 16
- erasure_strength: bfloat16 [65536, 1280], P(('dp', 'ctx')), parts along dimension 0, may hold values from 0 to 1
- forgetting_exponent: bfloat16 [65536, 1280], P(('dp', 'ctx')), parts along dimension 0, may hold values from -0.5 to 0
- initial_memory_matrix: float32 [1024, 1280], P('dp', 'ctx'), parts along dimension 0, may hold values from -384 to 384
- diagonal_boost_vector: float32 [1280], replicated, may hold values from -0.5 to 0.5
- layernorm_multiplier: float32 [1280], replicated, may hold values from 0.1 to 1.9
- layernorm_shift_vector: float32 [1280], replicated, may hold values from -2 to 2
Outputs:
- ungated_result: bfloat16 [65536, 1280], P(('dp', 'ctx')), parts along dimension 0
- exit_state: float32 [1024, 1280], P('dp', 'ctx'), parts along dimension 0
The draws below stay inside these ranges and needn't reach their ends.
There are 16 independent parts, one for each index of `dp`. The reference program is written for one: setup_inputs(seed, part) draws one part's arguments, and reference() takes and returns one part's arrays. A program takes and returns all parts, laid end to end along the dimension named above; an argument that names none is the same for every part. Nothing has to cross between parts.
All inputs are finite; a program needn't handle non-finite values.
Results may differ from the reference program's by a relative error of at most 0.001.
Values sent between devices are 32-bit elements; how exact they have to be, the bound alone decides.
No kernel may reach another device: no remote copies, remote signals or barrier semaphores. Data moves between devices by JAX's collectives and lax.ppermute only.
A program may use at most 128 MiB of HBM per device.

```python
import math
import jax
import jax.numpy as jnp
from jax import lax

DEVICE_SUBSPACES = 20
FEATURE_DIM = 64
TOK_DEV = 128
TOKENS = 4096


def slow_heads(key, share):
    picks = jax.random.uniform(jax.random.fold_in(key, 5), (DEVICE_SUBSPACES,))
    return jnp.repeat(picks < share, FEATURE_DIM)


def draw_forgetting_exponent(key, part):
    share = 0.5
    gradual_forgetting = slow_heads(key, share)
    key = jax.random.fold_in(key, 11)
    address_vectors = jax.random.split(key, 9)
    fast_life = jnp.exp(jax.random.uniform(address_vectors[0], (DEVICE_SUBSPACES,), minval=math.log(20.0), maxval=math.log(600.0)))
    slow_life = jnp.exp(jax.random.uniform(address_vectors[1], (DEVICE_SUBSPACES,), minval=math.log(2.0 * TOKENS), maxval=math.log(8.0 * TOKENS)))
    life = jnp.where(gradual_forgetting, jnp.repeat(slow_life, FEATURE_DIM), jnp.repeat(fast_life, FEATURE_DIM))
    rough = jax.random.uniform(address_vectors[2], (TOKENS, DEVICE_SUBSPACES * FEATURE_DIM), minval=0.5, maxval=1.5)
    factor = jnp.exp(jax.random.uniform(address_vectors[3], (TOKENS // TOK_DEV, DEVICE_SUBSPACES), minval=math.log(0.5), maxval=math.log(2.0)))
    factor = jnp.repeat(jnp.repeat(factor, TOK_DEV, axis=0), FEATURE_DIM, axis=1)
    starting_position = -rough * factor / life[None, :]
    places = jax.random.randint(address_vectors[4], (6,), 0, TOKENS)
    erased_memory = jnp.any(jnp.arange(TOKENS)[:, None] == places[None, :], axis=1)
    loss = jax.random.uniform(address_vectors[5], (TOKENS, DEVICE_SUBSPACES), minval=0.2, maxval=0.35)
    erased_component = jnp.log(1.0 - jnp.repeat(loss, FEATURE_DIM, axis=1))
    segment_span = jnp.where(erased_memory[:, None] & gradual_forgetting[None, :], erased_component, 0.0)
    combined = starting_position + segment_span
    block_length = min(128, TOKENS)
    block_count = TOKENS // block_length
    steep_head = jax.random.randint(address_vectors[6], (), 0, DEVICE_SUBSPACES)
    steep_block = jax.random.randint(address_vectors[7], (), 0, block_count)
    positions = jnp.arange(TOKENS)
    inside = positions // block_length == steep_block
    head_match = jnp.arange(DEVICE_SUBSPACES * FEATURE_DIM) // FEATURE_DIM == steep_head
    steep = -0.5 + 0.05 * jax.random.uniform(address_vectors[8], (TOKENS, DEVICE_SUBSPACES * FEATURE_DIM))
    steep = jnp.where((positions == steep_block * block_length)[:, None], -0.5, steep)
    combined = jnp.where(inside[:, None] & head_match[None, :], steep, combined)
    return combined.astype(jnp.bfloat16)


def draw_erasure_strength(key, part):
    key = jax.random.fold_in(key, 13)
    pieces = jax.random.split(key, 2)
    upper = min(1.0, 16.0 / min(128, TOK_DEV), 512.0 / TOKENS)
    spread = jax.random.uniform(pieces[0], (TOKENS, DEVICE_SUBSPACES * FEATURE_DIM)) * upper
    full_place = jnp.repeat(jax.random.randint(pieces[1], (DEVICE_SUBSPACES,), 0, TOKENS), FEATURE_DIM)
    spread = jnp.where(jnp.arange(TOKENS)[:, None] == full_place[None, :], 1.0, spread)
    return spread.astype(jnp.bfloat16)


def draw_erasure_vector_raw(key, part):
    key = jax.random.fold_in(key, 19)
    pieces = jax.random.split(key, 3)
    shared = jnp.clip(jax.random.normal(pieces[0], (DEVICE_SUBSPACES, FEATURE_DIM)), -4.0, 4.0)
    weight = jnp.exp(jax.random.uniform(pieces[1], (DEVICE_SUBSPACES,), minval=math.log(1.5), maxval=math.log(3.0)))
    leading = (shared * weight[:, None]).reshape(DEVICE_SUBSPACES * FEATURE_DIM)
    noise = jnp.clip(jax.random.normal(pieces[2], (TOKENS, DEVICE_SUBSPACES * FEATURE_DIM)), -4.0, 4.0)
    return jnp.clip(leading[None, :] + noise, -16.0, 16.0).astype(jnp.bfloat16)


def draw_content_matrix(key, part):
    key = jax.random.fold_in(key, 17)
    address_vectors = jax.random.split(key, 3)
    starting_position = jnp.clip(jax.random.normal(address_vectors[0], (TOKENS, DEVICE_SUBSPACES * FEATURE_DIM)), -4.0, 4.0)
    channel = jnp.exp(jax.random.uniform(address_vectors[1], (DEVICE_SUBSPACES * FEATURE_DIM,), minval=math.log(0.3), maxval=math.log(3.0)))
    rowscale = jnp.exp(jax.random.uniform(address_vectors[2], (TOKENS, 1), minval=math.log(0.5), maxval=math.log(2.0)))
    return (starting_position * channel[None, :] * rowscale).astype(jnp.bfloat16)


def shard_levels(key, shape, cuts, low, top_value):
    loudness, own = 1.0, jax.random.fold_in(key, 6)
    for dim, shards_of in cuts:
        draws = jnp.exp(jax.random.uniform(jax.random.fold_in(own, dim), (shards_of,), jnp.float32, low / len(cuts), top_value / len(cuts)))
        loudness = loudness * jnp.repeat(draws, shape[dim] // shards_of).reshape([-1 if axis == dim else 1 for axis in range(len(shape))])
    return loudness


def normal_values(rng, shape, deviation, limit, cuts=(), dtype=jnp.bfloat16):
    entries = jax.random.normal(rng, shape, jnp.float32) * deviation
    if len(cuts) > 0:
        entries = shard_levels(rng, shape, cuts, -0.22, 0.18) * entries
    return jnp.clip(entries, min=-limit, max=limit).astype(dtype)


def setup_inputs(seed: int = 0, part: int = 0) -> dict:
    seeds = jax.random.split(jax.random.key(seed), 11)
    own_keys = jax.random.split(jax.random.fold_in(seeds[10], part), 11)
    return {
        "query_matrix": normal_values(own_keys[0], (TOKENS, DEVICE_SUBSPACES * FEATURE_DIM), 1.0, 6.0, ((0, 32),)),
        "address_matrix": normal_values(own_keys[1], (TOKENS, DEVICE_SUBSPACES * FEATURE_DIM), 1.0, 6.0, ((0, 32),)),
        "content_matrix": draw_content_matrix(jax.random.fold_in(jax.random.fold_in(seeds[10], part), 71), part),
        "erasure_vector_raw": draw_erasure_vector_raw(jax.random.fold_in(jax.random.fold_in(seeds[10], part), 71), part),
        "erasure_strength": draw_erasure_strength(jax.random.fold_in(jax.random.fold_in(seeds[10], part), 71), part),
        "forgetting_exponent": draw_forgetting_exponent(jax.random.fold_in(jax.random.fold_in(seeds[10], part), 71), part),
        "initial_memory_matrix": normal_values(own_keys[6], (FEATURE_DIM, DEVICE_SUBSPACES * FEATURE_DIM), (TOKENS ** 0.5), 384.0, ((1, 32),), jnp.float32),
        "diagonal_boost_vector": normal_values(seeds[7], (DEVICE_SUBSPACES * FEATURE_DIM,), 0.1, 0.5, (), jnp.float32),
        "layernorm_multiplier": jnp.clip(1.0 + 0.18 * jax.random.normal(seeds[8], (DEVICE_SUBSPACES * FEATURE_DIM,), jnp.float32), 0.1, 1.9),
        "layernorm_shift_vector": normal_values(seeds[9], (DEVICE_SUBSPACES * FEATURE_DIM,), 0.3, 2.0, (), jnp.float32),
    }


def reference(query_matrix, address_matrix, content_matrix, erasure_vector_raw, erasure_strength, forgetting_exponent, initial_memory_matrix, diagonal_boost_vector, layernorm_multiplier, layernorm_shift_vector):
    highest_precision = lax.Precision.HIGHEST
    iteration_number = query_matrix.shape[0]

    def heads_of(x):
        return x.astype(jnp.float32).reshape(iteration_number, DEVICE_SUBSPACES, FEATURE_DIM)
    incoming_memory = heads_of(query_matrix)
    address_vectors = heads_of(address_matrix)
    content_vectors = heads_of(content_matrix)
    raw = heads_of(erasure_vector_raw)
    unit = raw * lax.rsqrt(lax.optimization_barrier(jnp.sum(raw * raw, axis=-1, keepdims=True)) + FEATURE_DIM * 1e-05)
    rates = heads_of(erasure_strength)
    decay = jnp.exp(heads_of(forgetting_exponent))
    start = initial_memory_matrix.astype(jnp.float32).reshape(FEATURE_DIM, DEVICE_SUBSPACES, FEATURE_DIM).transpose(1, 0, 2)

    def advance(running_state, inputs):
        receptance_row, k_row, v_row, update_row, a_row, w_row = inputs
        removed_part = jnp.einsum('sg,sgc->sc', update_row, running_state, precision=highest_precision)
        running_state = w_row[:, :, None] * running_state - (a_row * update_row)[:, :, None] * removed_part[:, None, :] + k_row[:, :, None] * v_row[:, None, :]
        return (running_state, jnp.einsum('sg,sgc->sc', receptance_row, running_state, precision=highest_precision))
    final, readout = lax.scan(advance, start, (incoming_memory, address_vectors, content_vectors, unit, rates, decay))
    mean = lax.optimization_barrier(jnp.mean(readout, axis=-1, keepdims=True))
    centred = readout - mean
    variance = lax.optimization_barrier(jnp.mean(centred * centred, axis=-1, keepdims=True))
    standardized_result = centred * lax.rsqrt(variance + 1e-05) * layernorm_multiplier.reshape(DEVICE_SUBSPACES, FEATURE_DIM) + layernorm_shift_vector.reshape(DEVICE_SUBSPACES, FEATURE_DIM)
    diagonal_contribution = lax.optimization_barrier(jnp.sum(incoming_memory * address_vectors * diagonal_boost_vector.reshape(DEVICE_SUBSPACES, FEATURE_DIM), axis=-1, keepdims=True)) * content_vectors
    ungated_result = (standardized_result + diagonal_contribution).reshape(iteration_number, DEVICE_SUBSPACES * FEATURE_DIM).astype(jnp.bfloat16)
    exit_state = final.transpose(1, 0, 2).reshape(FEATURE_DIM, DEVICE_SUBSPACES * FEATURE_DIM)
    return (ungated_result, exit_state)
```

```python
import functools

import jax
import jax.numpy as jnp
from jax import lax
from jax.experimental import pallas as pl
from jax.experimental.pallas import tpu as pltpu
from jax.sharding import PartitionSpec as P

HEADS = 20
CH = 64
PAIR = 2 * CH
PAIRS = HEADS // 2
WIDTH = HEADS * CH
GROUP = 5
INTERPRET = False
F32 = jnp.float32
BF16 = jnp.bfloat16
NN = (((1,), (0,)), ((), ()))
NT = (((1,), (1,)), ((), ()))


def mxu(a, b, dims=NN):
    return lax.dot_general(a, b, dims, preferred_element_type=F32)


def split(x):
    hi = x.astype(BF16)
    return hi, (x - hi.astype(F32)).astype(BF16)


def lanes(*xs):
    return jnp.concatenate(xs, axis=1)


def rows(*xs):
    return jnp.concatenate(xs, axis=0)


def square(a, b):
    both = lanes(*b)
    out = mxu(lanes(*a), rows(both, both))
    return out[:, :PAIR] + out[:, PAIR:]


def wide(a, b):
    return mxu(lanes(*a), rows(b[0], b[0])) + mxu(a[0], b[1])


def exact_right(a, b):
    return mxu(lanes(*a), rows(b, b))


def iota(shape, dim):
    return lax.broadcasted_iota(jnp.int32, shape, dim)


def low_half(n):
    return iota((n, PAIR), 1) < CH


def block_ones():
    same = (iota((PAIR, PAIR), 0) < CH) == (iota((PAIR, PAIR), 1) < CH)
    return jnp.where(same, 1.0, 0.0).astype(BF16)


def head_sum(x, ones):
    return exact_right(split(x), ones)


def decays(logs, tril):
    return mxu(tril, logs)


def units(raw, ones):
    raw = raw.astype(F32)
    return raw * lax.rsqrt(head_sum(raw * raw, ones) + CH * 1e-05)


def tril_ones(n):
    return jnp.where(iota((n, n), 0) >= iota((n, n), 1), 1.0, 0.0).astype(BF16)


def grams(left, right, low):
    zero = jnp.zeros_like(left)
    stacked = split(rows(jnp.where(low, left, zero), jnp.where(low, zero, left)))
    b = split(right)
    return mxu(lanes(*stacked), lanes(b[0], b[0]), NT) + mxu(stacked[0], b[1], NT)


def local_kernel(
    k_ref, v_ref, raw_ref, rate_ref, log_ref, slots_ref, w_ref, u_ref, moves, ends, *, owners, columns
):
    n = k_ref.shape[0]
    step = pl.program_id(0)
    low = low_half(n)
    ones = block_ones()
    tril = tril_ones(n)
    t_id, s_id = iota((n, n), 0), iota((n, n), 1)
    strict = t_id > s_id
    apart = t_id ^ s_id
    pairs = range(GROUP)
    cut = [slice(p * PAIR, (p + 1) * PAIR) for p in pairs]

    cumul = [decays(log_ref[:, c], tril) for c in cut]
    unit = [units(raw_ref[:, c], ones) for c in cut]
    alpha = [-unit[p] * jnp.exp(cumul[p] - log_ref[:, cut[p]].astype(F32)) for p in pairs]
    fall = [jnp.exp(-cumul[p]) for p in pairs]
    beta = [rate_ref[:, cut[p]].astype(F32) * unit[p] * fall[p] for p in pairs]
    key = [k_ref[:, cut[p]].astype(F32) * fall[p] for p in pairs]
    gram = [grams(alpha[p], rows(beta[p], key[p]), low) for p in pairs]

    heads = range(2 * GROUP)
    inner, cross = [], []
    for h in heads:
        part = gram[h // 2][(h % 2) * n : (h % 2 + 1) * n]
        inner.append(jnp.where(strict, part[:, :n], 0.0))
        cross.append(jnp.where(strict, part[:, n:], 0.0))
    akv = [exact_right(split(cross[h]), v_ref[:, cut[h // 2]]) for h in heads]
    akv = [jnp.where(low, akv[2 * p], akv[2 * p + 1]) for p in pairs]
    right = [split(lanes(alpha[p], akv[p])) for p in pairs]

    eye = jnp.where(t_id == s_id, 1.0, 0.0)
    solver = [eye + jnp.where(apart == 1, inner[h], 0.0) for h in heads]
    size = 2
    while size < n:
        joins = (apart >= size) & (apart < 2 * size)
        halves = [split(solver[h]) for h in heads]
        mid = [square(split(jnp.where(joins, inner[h], 0.0)), halves[h]) for h in heads]
        solver = [solver[h] + square(halves[h], split(mid[h])) for h in heads]
        size *= 2
    solved = [wide(split(solver[h]), right[h // 2]) for h in heads]
    for p in pairs:
        first, second = solved[2 * p], solved[2 * p + 1]
        w = jnp.where(low, first[:, :PAIR], second[:, :PAIR])
        u = jnp.where(low, first[:, PAIR:], second[:, PAIR:])
        w_ref[:, cut[p]] = w
        u_ref[:, cut[p]] = u
        scale = jnp.exp(cumul[p][n - 1 :, :])
        end_b = beta[p] * scale
        end_k = key[p] * scale
        moved = square(split(end_b.T), split(w))
        row, lane = iota((CH, PAIR), 0), iota((CH, PAIR), 1)
        diagonal = jnp.where(row == lane % CH, scale, 0.0)
        moves[step * GROUP + p] = jnp.where(low_half(CH), moved[:CH], moved[CH:]) + diagonal
        content = v_ref[:, cut[p]].astype(F32).T.astype(BF16)
        by_key = mxu(content, lanes(*split(end_k)))
        fresh = square(split(u.T), split(end_b)) + by_key[:, :PAIR] + by_key[:, PAIR:]
        own = (iota((PAIR, PAIR), 0) < CH) == low_half(PAIR)
        fresh = jnp.where(own, fresh, 0.0)
        ends[pl.ds(pl.multiple_of((step * GROUP + p) * PAIR, PAIR), PAIR), :] = fresh + pltpu.roll(
            fresh, CH, 1
        )

    @pl.when(step == pl.num_programs(0) - 1)
    def _():
        ends[WIDTH:, :] = jnp.zeros((ends.shape[0] - WIDTH, PAIR), F32)
        short = (columns + 15) // 16 * 8
        for owner in range(owners):
            first = owner * columns // CH
            if first % 2 == 0 or first == HEADS - 1:
                slot = moves[first // 2]
            else:
                slot = jnp.where(low_half(CH), moves[first // 2 + 1], moves[first // 2])
            slots_ref[owner, :CH, :] = slot
            at = owner * columns
            slots_ref[owner, CH:, :] = jnp.where(
                low_half(short), ends[at : at + short, :], ends[at + short : at + 2 * short, :]
            )


def read_kernel(
    q_ref, k_ref, v_ref, raw_ref, rate_ref, log_ref, w_ref, u_ref, boost_ref, shift_ref,
    read_ref, local_ref, base_ref,
):
    n = k_ref.shape[0]
    low = low_half(n)
    ones = block_ones()
    tril = tril_ones(n)
    weak = iota((n, n), 0) >= iota((n, n), 1)
    pairs = range(GROUP)
    cut = [slice(p * PAIR, (p + 1) * PAIR) for p in pairs]

    cumul = [decays(log_ref[:, c], tril) for c in cut]
    unit = [units(raw_ref[:, c], ones) for c in cut]
    fall = [jnp.exp(-cumul[p]) for p in pairs]
    beta = [rate_ref[:, cut[p]].astype(F32) * unit[p] * fall[p] for p in pairs]
    key = [k_ref[:, cut[p]].astype(F32) * fall[p] for p in pairs]
    read = [q_ref[:, cut[p]].astype(F32) * jnp.exp(cumul[p]) for p in pairs]
    gram = [grams(read[p], rows(beta[p], key[p]), low) for p in pairs]
    for p in pairs:
        c = cut[p]
        solved = split(lanes(w_ref[:, c], u_ref[:, c]))
        v = v_ref[:, c]
        reads, locals_ = [], []
        for h in range(2):
            part = gram[p][h * n : (h + 1) * n]
            both = wide(split(jnp.where(weak, part[:, :n], 0.0)), solved)
            direct = exact_right(split(jnp.where(weak, part[:, n:], 0.0)), v)
            reads.append(both[:, :PAIR])
            locals_.append(both[:, PAIR:] + direct)
        read_ref[:, c] = read[p] + jnp.where(low, *reads)
        local_ref[:, c] = jnp.where(low, *locals_)
        product = q_ref[:, c].astype(F32) * k_ref[:, c].astype(F32) * boost_ref[:, c]
        base_ref[:, c] = head_sum(product, ones) * v.astype(F32) + shift_ref[:, c]


def scan_kernel(slots_ref, entry_ref, mask_ref, starts_ref, exit_ref):
    short = starts_ref.shape[1]
    low = low_half(short)
    mask = mask_ref[...]
    state = entry_ref[...]
    for d in range(slots_ref.shape[0]):
        starts_ref[d] = jnp.where(low, state[:short], state[short:])
        hi, lo = split(slots_ref[d, :CH, :])
        weights = rows(lanes(hi, hi), lanes(hi, hi), lanes(lo, lo), lanes(lo, lo))
        end = slots_ref[d, CH:, :]
        turned = pltpu.roll(end, CH, 1)
        fresh = rows(jnp.where(low, end, turned), jnp.where(low, turned, end))
        out = mxu(lanes(*split(state * mask)), weights, NT)
        state = out[:, :PAIR] + out[:, PAIR:] + fresh
    exit_ref[...] = state


def final_kernel(starts_ref, read_ref, local_ref, base_ref, gain_ref, out_ref, begins, *, columns):
    short = starts_ref.shape[1]
    low = low_half(short)
    for owner in range(starts_ref.shape[0]):
        part = starts_ref[owner]
        turned = pltpu.roll(part, CH, 1)
        at = owner * columns
        begins[at : at + short, :] = jnp.where(low, part, turned)
        begins[at + short : at + columns, :] = jnp.where(low, turned, part)[: columns - short]
    own = (iota((PAIR, PAIR), 0) < CH) == low_half(PAIR)
    ones = block_ones()
    for p in range(PAIRS):
        c = slice(p * PAIR, (p + 1) * PAIR)
        a = split(read_ref[:, c])
        b = split(jnp.where(own, begins[c, :], 0.0))
        carried = mxu(lanes(*a), lanes(b[0], b[0]), NT) + mxu(a[0], b[1], NT)
        readout = carried + local_ref[:, c]
        centred = readout - head_sum(readout, ones) * (1.0 / CH)
        variance = head_sum(centred * centred, ones) * (1.0 / CH)
        scaled = centred * lax.rsqrt(variance + 1e-05) * gain_ref[:, c]
        out_ref[:, c] = (scaled + base_ref[:, c]).astype(BF16)


def call(kernel, **kwargs):
    params = pltpu.CompilerParams(vmem_limit_bytes=48 * 1024 * 1024)
    return pl.pallas_call(kernel, interpret=INTERPRET, compiler_params=params, **kwargs)


def shards(q, k, v, raw, rates, logs, memory, boost, gain, shift):
    n = q.shape[0]
    owners = lax.axis_size("ctx")
    columns = memory.shape[1]
    short = (columns + 15) // 16 * 8
    block = GROUP * PAIR
    tokens = pl.BlockSpec((n, block), lambda i: (0, i))
    vector = pl.BlockSpec((1, block), lambda i: (0, i))
    steps = WIDTH // block
    plane = jax.ShapeDtypeStruct((n, WIDTH), F32)

    slots, w, u = call(
        functools.partial(local_kernel, owners=owners, columns=columns),
        grid=(steps,),
        in_specs=[tokens] * 5,
        out_specs=[
            pl.BlockSpec((owners, CH + short, PAIR), lambda i: (0, 0, 0)),
            tokens,
            tokens,
        ],
        out_shape=[jax.ShapeDtypeStruct((owners, CH + short, PAIR), F32), plane, plane],
        scratch_shapes=[
            pltpu.VMEM((PAIRS, CH, PAIR), F32),
            pltpu.VMEM((WIDTH + 8, PAIR), F32),
        ],
    )(k, v, raw, rates, logs)
    slots = lax.all_to_all(slots, "ctx", 0, 0)

    read, local, base = call(
        read_kernel,
        grid=(steps,),
        in_specs=[tokens] * 8 + [vector] * 2,
        out_specs=[tokens] * 3,
        out_shape=[plane] * 3,
    )(q, k, v, raw, rates, logs, w, u, boost.reshape(1, WIDTH), shift.reshape(1, WIDTH))

    place = lax.axis_index("ctx")
    own = lax.broadcasted_iota(jnp.int32, (2 * short, PAIR), 0)
    half = lax.broadcasted_iota(jnp.int32, (2 * short, PAIR), 1) // CH
    mask = ((place * columns + own) // CH % 2 == half) & (own < columns)
    entry = jnp.pad(memory.T, ((0, 2 * short - columns), (0, 0)))
    starts, final = call(
        scan_kernel,
        out_shape=[
            jax.ShapeDtypeStruct((owners, short, PAIR), F32),
            jax.ShapeDtypeStruct((2 * short, PAIR), F32),
        ],
    )(slots, jnp.concatenate([entry, entry], axis=1), mask.astype(F32))
    starts = lax.all_to_all(starts, "ctx", 0, 0)
    exit_state = final[:columns, :CH].T

    out = call(
        functools.partial(final_kernel, columns=columns),
        out_shape=jax.ShapeDtypeStruct((n, WIDTH), BF16),
        scratch_shapes=[pltpu.VMEM((WIDTH, PAIR), F32)],
    )(starts, read, local, base, gain.reshape(1, WIDTH))
    return out, exit_state


def solution(mesh):
    rows_spec = P(("dp", "ctx"), None)
    return jax.shard_map(
        shards,
        mesh=mesh,
        in_specs=(rows_spec,) * 6 + (P("dp", "ctx"), P(), P(), P()),
        out_specs=(rows_spec, P("dp", "ctx")),
        check_vma=False,
    )
```

```python
import functools

import jax
import jax.numpy as jnp
from jax import lax
from jax.experimental import pallas as pl
from jax.experimental.pallas import tpu as pltpu
from jax.sharding import PartitionSpec as P

HEADS = 20
CH = 64
PAIR = 2 * CH
PAIRS = HEADS // 2
WIDTH = HEADS * CH
GROUP = 5
INTERPRET = False
F32 = jnp.float32
BF16 = jnp.bfloat16
NN = (((1,), (0,)), ((), ()))
NT = (((1,), (1,)), ((), ()))


def mxu(a, b, dims=NN):
    return lax.dot_general(a, b, dims, preferred_element_type=F32)


def split(x):
    hi = x.astype(BF16)
    return hi, (x - hi.astype(F32)).astype(BF16)


def lanes(*xs):
    return jnp.concatenate(xs, axis=1)


def rows(*xs):
    return jnp.concatenate(xs, axis=0)


def square(a, b):
    both = lanes(*b)
    out = mxu(lanes(*a), rows(both, both))
    return out[:, :PAIR] + out[:, PAIR:]


def wide(a, b):
    return mxu(lanes(*a), rows(b[0], b[0])) + mxu(a[0], b[1])


def exact_right(a, b):
    return mxu(lanes(*a), rows(b, b))


def iota(shape, dim):
    return lax.broadcasted_iota(jnp.int32, shape, dim)


def low_half(n):
    return iota((n, PAIR), 1) < CH


def block_ones():
    same = (iota((PAIR, PAIR), 0) < CH) == (iota((PAIR, PAIR), 1) < CH)
    return jnp.where(same, 1.0, 0.0).astype(BF16)


def head_sum(x, ones):
    return exact_right(split(x), ones)


def decays(logs, tril):
    return mxu(tril, logs)


def units(raw, ones):
    raw = raw.astype(F32)
    return raw * lax.rsqrt(head_sum(raw * raw, ones) + CH * 1e-05)


def tril_ones(n):
    return jnp.where(iota((n, n), 0) >= iota((n, n), 1), 1.0, 0.0).astype(BF16)


def grams(left, right, low):
    zero = jnp.zeros_like(left)
    stacked = split(rows(jnp.where(low, left, zero), jnp.where(low, zero, left)))
    b = split(right)
    return mxu(lanes(*stacked), lanes(b[0], b[0]), NT) + mxu(stacked[0], b[1], NT)


def inverse(inner):
    n = inner[0].shape[0]
    slab = 16
    count = n // slab
    row, lane = iota((slab, n), 0), iota((slab, n), 1)
    apart = row ^ (lane % slab)
    same = jnp.where(iota((n, n), 0) // slab == iota((n, n), 1) // slab, 1.0, 0.0)
    same_short = same.astype(BF16)

    def spread(pair):
        return tuple(rows(*[x] * count) * same_short for x in pair)

    small = [sum(jnp.where(lane // slab == i, x[i * slab : (i + 1) * slab], 0.0) for i in range(count)) for x in inner]
    solver = [jnp.where(apart == 0, 1.0, 0.0) + jnp.where(apart == 1, x, 0.0) for x in small]
    size = 2
    while size < slab:
        joins = (apart >= size) & (apart < 2 * size)
        halves = [split(x) for x in solver]
        mid = [square(split(jnp.where(joins, x, 0.0)), spread(t)) for x, t in zip(small, halves)]
        solver = [x + square(t, spread(split(m))) for x, t, m in zip(solver, halves, mid)]
        size *= 2
    halves = [spread(split(x)) for x in solver]
    solver = [rows(*[x] * count) * same for x in solver]

    while size < n:
        odd = lambda x: rows(*[x[i : i + size] for i in range(size, n, 2 * size)])

        def joined(even_of, new):
            parts = []
            for i in range(0, n // 2, size):
                parts += [even_of(2 * i), new[i : i + size]]
            return rows(*parts)

        apart = odd(iota((n, n), 0) ^ iota((n, n), 1))
        joins = (apart >= size) & (apart < 2 * size)
        gap = jnp.zeros((size, n), BF16)
        mid = [square(split(jnp.where(joins, odd(x), 0.0)), t) for x, t in zip(inner, halves)]
        mid = [tuple(joined(lambda i: gap, m) for m in split(x)) for x in mid]
        later = [
            odd(x) + square((odd(t[0]), odd(t[1])), m) for x, t, m in zip(solver, halves, mid)
        ]
        halves = [
            tuple(joined(lambda i: old[i : i + size], new) for old, new in zip(t, split(x)))
            for x, t in zip(later, halves)
        ]
        solver = [joined(lambda i: x[i : i + size], y) for x, y in zip(solver, later)]
        size *= 2
    return halves


def local_kernel(*refs, owners, columns):
    inputs, (slots_out, w_out, u_out) = refs[:5], refs[5:8]
    buffers = refs[8:13]
    slots, w_all, u_all, ends, in_sems, out_sems = refs[13:]
    n, width = w_all.shape
    block = GROUP * PAIR
    groups = width // block
    loads = [
        [
            pltpu.make_async_copy(src.at[:, pl.ds(g * block, block)], dst.at[:, pl.ds(g * block, block)], in_sems.at[g, i])
            for i, (src, dst) in enumerate(zip(inputs, buffers))
        ]
        for g in range(groups)
    ]
    for group in loads:
        for copy in group:
            copy.start()
    k_ref, v_ref, raw_ref, rate_ref, log_ref = buffers
    low = low_half(n)
    ones = block_ones()
    tril = tril_ones(n)
    strict = iota((n, n), 0) > iota((n, n), 1)
    own = (iota((PAIR, PAIR), 0) < CH) == low_half(PAIR)
    short = (columns + 15) // 16 * 8
    row, lane = iota((CH, PAIR), 0), iota((CH, PAIR), 1)
    moves, stores, owner = [], [], 0
    pairs = range(GROUP)
    heads = range(2 * GROUP)
    for g in range(groups):
        for copy in loads[g]:
            copy.wait()
        cut = [slice(g * block + p * PAIR, g * block + (p + 1) * PAIR) for p in pairs]
        cumul = [decays(log_ref[:, c], tril) for c in cut]
        unit = [units(raw_ref[:, c], ones) for c in cut]
        alpha = [-unit[p] * jnp.exp(cumul[p] - log_ref[:, cut[p]].astype(F32)) for p in pairs]
        fall = [jnp.exp(-cumul[p]) for p in pairs]
        beta = [rate_ref[:, cut[p]].astype(F32) * unit[p] * fall[p] for p in pairs]
        key = [k_ref[:, cut[p]].astype(F32) * fall[p] for p in pairs]
        gram = [grams(alpha[p], rows(beta[p], key[p]), low) for p in pairs]

        inner, cross = [], []
        for h in heads:
            part = gram[h // 2][(h % 2) * n : (h % 2 + 1) * n]
            inner.append(jnp.where(strict, part[:, :n], 0.0))
            cross.append(jnp.where(strict, part[:, n:], 0.0))
        akv = [exact_right(split(cross[h]), v_ref[:, cut[h // 2]]) for h in heads]
        akv = [jnp.where(low, akv[2 * p], akv[2 * p + 1]) for p in pairs]
        right = [split(lanes(alpha[p], akv[p])) for p in pairs]
        solver = inverse(inner)
        solved = [wide(solver[h], right[h // 2]) for h in heads]
        for p in pairs:
            first, second = solved[2 * p], solved[2 * p + 1]
            w = jnp.where(low, first[:, :PAIR], second[:, :PAIR])
            u = jnp.where(low, first[:, PAIR:], second[:, PAIR:])
            w_all[:, cut[p]] = w
            u_all[:, cut[p]] = u
            scale = jnp.exp(cumul[p][n - 1 :, :])
            end_b = beta[p] * scale
            end_k = key[p] * scale
            moved = square(split(end_b.T), split(w))
            diagonal = jnp.where(row == lane % CH, scale, 0.0)
            moves.append(jnp.where(low_half(CH), moved[:CH], moved[CH:]) + diagonal)
            content = v_ref[:, cut[p]].astype(F32).T.astype(BF16)
            by_key = mxu(content, lanes(*split(end_k)))
            fresh = square(split(u.T), split(end_b)) + by_key[:, :PAIR] + by_key[:, PAIR:]
            fresh = jnp.where(own, fresh, 0.0)
            ends[cut[p], :] = fresh + pltpu.roll(fresh, CH, 1)

        begin = owner
        while owner < owners and (owner + 1) * columns <= (g + 1) * block:
            at = owner * columns
            first, last = at // CH, (at + columns - 1) // CH
            slot = moves[first // 2]
            if first // 2 != last // 2:
                slot = jnp.where(low_half(CH), moves[last // 2], slot)
            slots[owner, :CH, :] = slot
            tail = rows(ends[at + short : at + columns, :], jnp.zeros((2 * short - columns, PAIR), F32))
            slots[owner, CH:, :] = jnp.where(low_half(short), ends[at : at + short, :], tail)
            owner += 1
        here = pl.ds(g * block, block)
        ready = pl.ds(begin, owner - begin)
        stores += [
            pltpu.make_async_copy(slots.at[ready], slots_out.at[ready], out_sems.at[g, 0]),
            pltpu.make_async_copy(w_all.at[:, here], w_out.at[:, here], out_sems.at[g, 1]),
            pltpu.make_async_copy(u_all.at[:, here], u_out.at[:, here], out_sems.at[g, 2]),
        ]
        for copy in stores[-3:]:
            copy.start()
    for copy in stores:
        copy.wait()


def read_kernel(*refs):
    inputs, (boost_ref, shift_ref) = refs[:8], refs[8:10]
    outputs = refs[10:13]
    buffers = refs[13:21]
    results, in_sems, out_sems = refs[21:24], refs[24], refs[25]
    n, width = results[0].shape
    block = GROUP * PAIR
    groups = width // block

    def moved(sources, targets, sems, g):
        here = pl.ds(g * block, block)
        return [
            pltpu.make_async_copy(src.at[:, here], dst.at[:, here], sems.at[g, i])
            for i, (src, dst) in enumerate(zip(sources, targets))
        ]

    loads = [moved(inputs, buffers, in_sems, g) for g in range(groups)]
    for group in loads:
        for copy in group:
            copy.start()
    q_ref, k_ref, v_ref, raw_ref, rate_ref, log_ref, w_ref, u_ref = buffers
    read_ref, local_ref, base_ref = results
    low = low_half(n)
    ones = block_ones()
    tril = tril_ones(n)
    weak = iota((n, n), 0) >= iota((n, n), 1)
    pairs = range(GROUP)
    stores = []
    for g in range(groups):
        for copy in loads[g]:
            copy.wait()
        cut = [slice(g * block + p * PAIR, g * block + (p + 1) * PAIR) for p in pairs]
        cumul = [decays(log_ref[:, c], tril) for c in cut]
        unit = [units(raw_ref[:, c], ones) for c in cut]
        fall = [jnp.exp(-cumul[p]) for p in pairs]
        beta = [rate_ref[:, cut[p]].astype(F32) * unit[p] * fall[p] for p in pairs]
        key = [k_ref[:, cut[p]].astype(F32) * fall[p] for p in pairs]
        read = [q_ref[:, cut[p]].astype(F32) * jnp.exp(cumul[p]) for p in pairs]
        gram = [grams(read[p], rows(beta[p], key[p]), low) for p in pairs]
        for p in pairs:
            c = cut[p]
            solved = split(lanes(w_ref[:, c], u_ref[:, c]))
            v = v_ref[:, c]
            reads, locals_ = [], []
            for h in range(2):
                part = gram[p][h * n : (h + 1) * n]
                both = wide(split(jnp.where(weak, part[:, :n], 0.0)), solved)
                direct = exact_right(split(jnp.where(weak, part[:, n:], 0.0)), v)
                reads.append(both[:, :PAIR])
                locals_.append(both[:, PAIR:] + direct)
            read_ref[:, c] = read[p] + jnp.where(low, *reads)
            local_ref[:, c] = jnp.where(low, *locals_)
            product = q_ref[:, c].astype(F32) * k_ref[:, c].astype(F32) * boost_ref[:, c]
            base_ref[:, c] = head_sum(product, ones) * v.astype(F32) + shift_ref[:, c]
        stores += moved(results, outputs, out_sems, g)
        for copy in stores[-3:]:
            copy.start()
    for copy in stores:
        copy.wait()


def scan_kernel(slots_ref, entry_ref, mask_ref, after_ref, starts_out, exit_ref, starts, sems):
    del after_ref
    count, short = starts.shape[:2]
    low = low_half(short)
    mask = mask_ref[...]
    state = entry_ref[...]
    chunk = count // sems.shape[0]
    stores = []
    for d in range(count):
        starts[d] = jnp.where(low, state[:short], state[short:])
        if d % chunk == chunk - 1:
            part = pl.ds(d + 1 - chunk, chunk)
            stores.append(pltpu.make_async_copy(starts.at[part], starts_out.at[part], sems.at[d // chunk]))
            stores[-1].start()
        hi, lo = split(slots_ref[d, :CH, :])
        weights = rows(lanes(hi, hi), lanes(hi, hi), lanes(lo, lo), lanes(lo, lo))
        end = slots_ref[d, CH:, :]
        turned = pltpu.roll(end, CH, 1)
        fresh = rows(jnp.where(low, end, turned), jnp.where(low, turned, end))
        out = mxu(lanes(*split(state * mask)), weights, NT)
        state = out[:, :PAIR] + out[:, PAIR:] + fresh
    exit_ref[...] = state
    for copy in stores:
        copy.wait()


def final_kernel(starts_ref, read_in, local_in, base_in, gain_ref, out, *scratch, columns):
    buffers, (begins, result, in_sems, out_sems) = scratch[:3], scratch[3:]
    read_ref, local_ref, base_ref = buffers
    cut = [slice(p * PAIR, (p + 1) * PAIR) for p in range(PAIRS)]
    place = [pl.ds(p * PAIR, PAIR) for p in range(PAIRS)]
    block = GROUP * PAIR
    loads = []
    for g in range(WIDTH // block):
        here = pl.ds(g * block, block)
        for i, (src, dst) in enumerate(zip((read_in, local_in, base_in), buffers)):
            loads.append(pltpu.make_async_copy(src.at[:, here], dst.at[:, here], in_sems.at[g, i]))
    for copy in loads:
        copy.start()
    short = starts_ref.shape[1]
    low = low_half(short)
    for owner in range(starts_ref.shape[0]):
        part = starts_ref[owner]
        turned = pltpu.roll(part, CH, 1)
        at = owner * columns
        begins[at : at + short, :] = jnp.where(low, part, turned)
        begins[at + short : at + columns, :] = jnp.where(low, turned, part)[: columns - short]
    own = (iota((PAIR, PAIR), 0) < CH) == low_half(PAIR)
    ones = block_ones()
    right = [split(jnp.where(own, begins[c, :], 0.0)) for c in cut]
    stores = []
    for g in range(PAIRS // GROUP):
        for copy in loads[3 * g : 3 * g + 3]:
            copy.wait()
        pairs = range(g * GROUP, (g + 1) * GROUP)
        left = [split(read_ref[:, cut[p]]) for p in pairs]
        carried = [
            mxu(lanes(*a), lanes(right[p][0], right[p][0]), NT) + mxu(a[0], right[p][1], NT)
            for p, a in zip(pairs, left)
        ]
        readout = [x + local_ref[:, cut[p]] for p, x in zip(pairs, carried)]
        centred = [x - head_sum(x, ones) * (1.0 / CH) for x in readout]
        variance = [head_sum(x * x, ones) * (1.0 / CH) for x in centred]
        for p, x, y in zip(pairs, centred, variance):
            scaled = x * lax.rsqrt(y + 1e-05) * gain_ref[:, cut[p]]
            result[:, cut[p]] = (scaled + base_ref[:, cut[p]]).astype(BF16)
            stores.append(pltpu.make_async_copy(result.at[:, place[p]], out.at[:, place[p]], out_sems.at[p]))
            stores[-1].start()
    for copy in stores:
        copy.wait()


def call(kernel, **kwargs):
    params = pltpu.CompilerParams(vmem_limit_bytes=48 * 1024 * 1024)
    return pl.pallas_call(kernel, interpret=INTERPRET, compiler_params=params, **kwargs)


def shards(q, k, v, raw, rates, logs, memory, boost, gain, shift):
    n = q.shape[0]
    owners = lax.axis_size("ctx")
    columns = memory.shape[1]
    short = (columns + 15) // 16 * 8
    groups = PAIRS // GROUP
    hbm = pl.BlockSpec(memory_space=pltpu.HBM)
    vmem = pl.BlockSpec(memory_space=pltpu.VMEM)
    plane = jax.ShapeDtypeStruct((n, WIDTH), F32)
    tokens = pltpu.VMEM((n, WIDTH), BF16)
    floats = pltpu.VMEM((n, WIDTH), F32)
    sems = pltpu.SemaphoreType.DMA

    slots, w, u = call(
        functools.partial(local_kernel, owners=owners, columns=columns),
        in_specs=[hbm] * 5,
        out_specs=[hbm] * 3,
        out_shape=[jax.ShapeDtypeStruct((owners, CH + short, PAIR), F32), plane, plane],
        scratch_shapes=[tokens] * 5
        + [
            pltpu.VMEM((owners, CH + short, PAIR), F32),
            floats,
            floats,
            pltpu.VMEM((WIDTH, PAIR), F32),
            sems((groups, 5)),
            sems((groups, 3)),
        ],
    )(k, v, raw, rates, logs)
    slots = lax.all_to_all(slots, "ctx", 0, 0)

    read, local, base = call(
        read_kernel,
        in_specs=[hbm] * 8 + [vmem] * 2,
        out_specs=[hbm] * 3,
        out_shape=[plane] * 3,
        scratch_shapes=[tokens] * 6 + [floats] * 5 + [sems((groups, 8)), sems((groups, 3))],
    )(q, k, v, raw, rates, logs, w, u, boost.reshape(1, WIDTH), shift.reshape(1, WIDTH))

    place = lax.axis_index("ctx")
    own = lax.broadcasted_iota(jnp.int32, (2 * short, PAIR), 0)
    half = lax.broadcasted_iota(jnp.int32, (2 * short, PAIR), 1) // CH
    mask = ((place * columns + own) // CH % 2 == half) & (own < columns)
    entry = jnp.pad(memory.T, ((0, 2 * short - columns), (0, 0)))
    starts, final = call(
        scan_kernel,
        in_specs=[vmem, vmem, vmem, hbm],
        out_specs=[hbm, vmem],
        out_shape=[
            jax.ShapeDtypeStruct((owners, short, PAIR), F32),
            jax.ShapeDtypeStruct((2 * short, PAIR), F32),
        ],
        scratch_shapes=[pltpu.VMEM((owners, short, PAIR), F32), sems((4,))],
    )(slots, jnp.concatenate([entry, entry], axis=1), mask.astype(F32), base)
    starts = lax.all_to_all(starts, "ctx", 0, 0)
    exit_state = final[:columns, :CH].T

    out = call(
        functools.partial(final_kernel, columns=columns),
        in_specs=[vmem, hbm, hbm, hbm, vmem],
        out_specs=hbm,
        out_shape=jax.ShapeDtypeStruct((n, WIDTH), BF16),
        scratch_shapes=[floats] * 3
        + [pltpu.VMEM((WIDTH, PAIR), F32), tokens, sems((groups, 3)), sems((PAIRS,))],
    )(starts, read, local, base, gain.reshape(1, WIDTH))
    return out, exit_state


def solution(mesh):
    rows_spec = P(("dp", "ctx"), None)
    return jax.shard_map(
        shards,
        mesh=mesh,
        in_specs=(rows_spec,) * 6 + (P("dp", "ctx"), P(), P(), P()),
        out_specs=(rows_spec, P("dp", "ctx")),
        check_vma=False,
    )
```

```python
import functools

import jax
import jax.numpy as jnp
from jax import lax
from jax.experimental import pallas as pl
from jax.experimental.pallas import tpu as pltpu
from jax.sharding import PartitionSpec as P

HEADS = 20
CH = 64
PAIR = 2 * CH
PAIRS = HEADS // 2
WIDTH = HEADS * CH
GROUP = 5
INTERPRET = False
F32 = jnp.float32
BF16 = jnp.bfloat16
NN = (((1,), (0,)), ((), ()))
NT = (((1,), (1,)), ((), ()))


def mxu(a, b, dims=NN):
    return lax.dot_general(a, b, dims, preferred_element_type=F32)


def split(x):
    hi = x.astype(BF16)
    return hi, (x - hi.astype(F32)).astype(BF16)


def lanes(*xs):
    return jnp.concatenate(xs, axis=1)


def rows(*xs):
    return jnp.concatenate(xs, axis=0)


def square(a, b):
    both = lanes(*b)
    out = mxu(lanes(*a), rows(both, both))
    return out[:, :PAIR] + out[:, PAIR:]


def wide(a, b):
    return mxu(lanes(*a), rows(b[0], b[0])) + mxu(a[0], b[1])


def exact_right(a, b):
    return mxu(lanes(*a), rows(b, b))


def iota(shape, dim):
    return lax.broadcasted_iota(jnp.int32, shape, dim)


def low_half(n):
    return iota((n, PAIR), 1) < CH


def block_ones():
    same = (iota((PAIR, PAIR), 0) < CH) == (iota((PAIR, PAIR), 1) < CH)
    return jnp.where(same, 1.0, 0.0).astype(BF16)


def head_sum(x, ones):
    return exact_right(split(x), ones)


def decays(logs, tril):
    return mxu(tril, logs)


def units(raw, ones):
    raw = raw.astype(F32)
    return raw * lax.rsqrt(head_sum(raw * raw, ones) + CH * 1e-05)


def tril_ones(n):
    return jnp.where(iota((n, n), 0) >= iota((n, n), 1), 1.0, 0.0).astype(BF16)


def grams(left, right, low):
    zero = jnp.zeros_like(left)
    stacked = split(rows(jnp.where(low, left, zero), jnp.where(low, zero, left)))
    b = split(right)
    return mxu(lanes(*stacked), lanes(b[0], b[0]), NT) + mxu(stacked[0], b[1], NT)


def inverse(inner):
    n = inner[0].shape[0]
    slab = 16
    count = n // slab
    row, lane = iota((slab, n), 0), iota((slab, n), 1)
    apart = row ^ (lane % slab)
    same = jnp.where(iota((n, n), 0) // slab == iota((n, n), 1) // slab, 1.0, 0.0)
    same_short = same.astype(BF16)

    def spread(pair):
        return tuple(rows(*[x] * count) * same_short for x in pair)

    small = [sum(jnp.where(lane // slab == i, x[i * slab : (i + 1) * slab], 0.0) for i in range(count)) for x in inner]
    solver = [jnp.where(apart == 0, 1.0, 0.0) + jnp.where(apart == 1, x, 0.0) for x in small]
    size = 2
    while size < slab:
        joins = (apart >= size) & (apart < 2 * size)
        halves = [split(x) for x in solver]
        mid = [square(split(jnp.where(joins, x, 0.0)), spread(t)) for x, t in zip(small, halves)]
        solver = [x + square(t, spread(split(m))) for x, t, m in zip(solver, halves, mid)]
        size *= 2
    halves = [spread(split(x)) for x in solver]
    solver = [rows(*[x] * count) * same for x in solver]

    while size < n:
        odd = lambda x: rows(*[x[i : i + size] for i in range(size, n, 2 * size)])

        def joined(even_of, new):
            parts = []
            for i in range(0, n // 2, size):
                parts += [even_of(2 * i), new[i : i + size]]
            return rows(*parts)

        apart = odd(iota((n, n), 0) ^ iota((n, n), 1))
        joins = (apart >= size) & (apart < 2 * size)
        gap = jnp.zeros((size, n), BF16)
        mid = [square(split(jnp.where(joins, odd(x), 0.0)), t) for x, t in zip(inner, halves)]
        mid = [tuple(joined(lambda i: gap, m) for m in split(x)) for x in mid]
        later = [
            odd(x) + square((odd(t[0]), odd(t[1])), m) for x, t, m in zip(solver, halves, mid)
        ]
        halves = [
            tuple(joined(lambda i: old[i : i + size], new) for old, new in zip(t, split(x)))
            for x, t in zip(later, halves)
        ]
        solver = [joined(lambda i: x[i : i + size], y) for x, y in zip(solver, later)]
        size *= 2
    return halves


def local_kernel(*refs):
    inputs, (pieces_out, w_out, u_out) = refs[:5], refs[5:8]
    buffers = refs[8:13]
    pieces, w_all, u_all, in_sems, out_sems = refs[13:]
    n, width = w_all.shape
    block = GROUP * PAIR
    groups = width // block
    loads = [
        [
            pltpu.make_async_copy(src.at[:, pl.ds(g * block, block)], dst.at[:, pl.ds(g * block, block)], in_sems.at[g, i])
            for i, (src, dst) in enumerate(zip(inputs, buffers))
        ]
        for g in range(groups)
    ]
    for group in loads:
        for copy in group:
            copy.start()
    k_ref, v_ref, raw_ref, rate_ref, log_ref = buffers
    low = low_half(n)
    ones = block_ones()
    tril = tril_ones(n)
    strict = iota((n, n), 0) > iota((n, n), 1)
    row, lane = iota((CH, PAIR), 0), iota((CH, PAIR), 1)
    stores = []
    pairs = range(GROUP)
    heads = range(2 * GROUP)
    for g in range(groups):
        for copy in loads[g]:
            copy.wait()
        cut = [slice(g * block + p * PAIR, g * block + (p + 1) * PAIR) for p in pairs]
        cumul = [decays(log_ref[:, c], tril) for c in cut]
        unit = [units(raw_ref[:, c], ones) for c in cut]
        alpha = [-unit[p] * jnp.exp(cumul[p] - log_ref[:, cut[p]].astype(F32)) for p in pairs]
        fall = [jnp.exp(-cumul[p]) for p in pairs]
        beta = [rate_ref[:, cut[p]].astype(F32) * unit[p] * fall[p] for p in pairs]
        key = [k_ref[:, cut[p]].astype(F32) * fall[p] for p in pairs]
        gram = [grams(alpha[p], rows(beta[p], key[p]), low) for p in pairs]

        inner, cross = [], []
        for h in heads:
            part = gram[h // 2][(h % 2) * n : (h % 2 + 1) * n]
            inner.append(jnp.where(strict, part[:, :n], 0.0))
            cross.append(jnp.where(strict, part[:, n:], 0.0))
        akv = [exact_right(split(cross[h]), v_ref[:, cut[h // 2]]) for h in heads]
        akv = [jnp.where(low, akv[2 * p], akv[2 * p + 1]) for p in pairs]
        right = [split(lanes(alpha[p], akv[p])) for p in pairs]
        solver = inverse(inner)
        solved = [wide(solver[h], right[h // 2]) for h in heads]
        for p in pairs:
            first, second = solved[2 * p], solved[2 * p + 1]
            w = jnp.where(low, first[:, :PAIR], second[:, :PAIR])
            u = jnp.where(low, first[:, PAIR:], second[:, PAIR:])
            w_all[:, cut[p]] = w
            u_all[:, cut[p]] = u
            scale = jnp.exp(cumul[p][n - 1 :, :])
            end_b = beta[p] * scale
            end_k = key[p] * scale
            moved = square(split(end_b.T), split(w))
            diagonal = jnp.where(row == lane % CH, scale, 0.0)
            pieces[0, g * GROUP + p] = jnp.where(low_half(CH), moved[:CH], moved[CH:]) + diagonal
            content = v_ref[:, cut[p]].astype(F32).T.astype(BF16)
            by_key = mxu(content, lanes(*split(end_k)))
            fresh = square(split(u.T), split(end_b)) + by_key[:, :PAIR] + by_key[:, PAIR:]
            pieces[1, g * GROUP + p] = jnp.where(low_half(CH), fresh[:CH], fresh[CH:])

        here = pl.ds(g * block, block)
        ready = pl.ds(g * GROUP, GROUP)
        stores += [
            pltpu.make_async_copy(pieces.at[:, ready], pieces_out.at[:, ready], out_sems.at[g, 0]),
            pltpu.make_async_copy(w_all.at[:, here], w_out.at[:, here], out_sems.at[g, 1]),
            pltpu.make_async_copy(u_all.at[:, here], u_out.at[:, here], out_sems.at[g, 2]),
        ]
        for copy in stores[-3:]:
            copy.start()
    for copy in stores:
        copy.wait()


def diagonal_blocks(x):
    own = (iota((PAIR, PAIR), 0) < CH) == low_half(PAIR)
    return jnp.where(own, rows(x, x), 0.0)


def square_nt(a, b):
    out = mxu(lanes(*a), rows(lanes(b[0], b[0]), lanes(b[1], b[1])), NT)
    return out[:, :PAIR] + out[:, PAIR:]


def compose_kernel(mine_ref, other_ref, late_ref, slots_ref, moves, ends, *, columns):
    late = late_ref[...] > 0.5
    low = low_half(CH)
    short = (columns + 15) // 16 * 8
    for p in range(PAIRS):
        mine, other = mine_ref[0, p], other_ref[0, p]
        first, second = jnp.where(late, other, mine), jnp.where(late, mine, other)
        moves[p] = square(split(second), split(diagonal_blocks(first)))
        mine, other = mine_ref[1, p], other_ref[1, p]
        first, end = jnp.where(late, other, mine), jnp.where(late, mine, other)
        end = end + square_nt(split(first), split(diagonal_blocks(second)))
        turned = pltpu.roll(end, CH, 1)
        ends[p * PAIR : p * PAIR + CH, :] = jnp.where(low, end, turned)
        ends[p * PAIR + CH : (p + 1) * PAIR, :] = jnp.where(low, turned, end)

    def packed(owner):
        at = owner * columns
        first, last = at // CH, (at + columns - 1) // CH
        slot = moves[first // 2]
        if first // 2 != last // 2:
            slot = jnp.where(low, moves[last // 2], slot)
        tail = rows(ends[at + short : at + columns, :], jnp.zeros((2 * short - columns, PAIR), F32))
        return slot, jnp.where(low_half(short), ends[at : at + short, :], tail)

    for chip in range(slots_ref.shape[0]):
        (move_a, end_a), (move_b, end_b) = packed(2 * chip), packed(2 * chip + 1)
        slots_ref[chip, :CH, :] = jnp.where(late, move_b, move_a)
        slots_ref[chip, CH:, :] = jnp.where(late, end_b, end_a)


def read_kernel(*refs):
    inputs, (boost_ref, shift_ref, other_ref, late_ref) = refs[:8], refs[8:12]
    outputs = refs[12:15]
    buffers = refs[15:23]
    results, in_sems, out_sems = refs[23:26], refs[26], refs[27]
    n, width = results[0].shape
    block = GROUP * PAIR
    groups = width // block

    def moved(sources, targets, sems, g):
        here = pl.ds(g * block, block)
        return [
            pltpu.make_async_copy(src.at[:, here], dst.at[:, here], sems.at[g, i])
            for i, (src, dst) in enumerate(zip(sources, targets))
        ]

    loads = [moved(inputs, buffers, in_sems, g) for g in range(groups)]
    for group in loads:
        for copy in group:
            copy.start()
    q_ref, k_ref, v_ref, raw_ref, rate_ref, log_ref, w_ref, u_ref = buffers
    read_ref, local_ref, base_ref = results
    low = low_half(n)
    ones = block_ones()
    tril = tril_ones(n)
    weak = iota((n, n), 0) >= iota((n, n), 1)
    late = late_ref[...] > 0.5
    pairs = range(GROUP)
    stores = []
    for g in range(groups):
        for copy in loads[g]:
            copy.wait()
        cut = [slice(g * block + p * PAIR, g * block + (p + 1) * PAIR) for p in pairs]
        cumul = [decays(log_ref[:, c], tril) for c in cut]
        unit = [units(raw_ref[:, c], ones) for c in cut]
        fall = [jnp.exp(-cumul[p]) for p in pairs]
        beta = [rate_ref[:, cut[p]].astype(F32) * unit[p] * fall[p] for p in pairs]
        key = [k_ref[:, cut[p]].astype(F32) * fall[p] for p in pairs]
        read = [q_ref[:, cut[p]].astype(F32) * jnp.exp(cumul[p]) for p in pairs]
        gram = [grams(read[p], rows(beta[p], key[p]), low) for p in pairs]
        for p in pairs:
            c = cut[p]
            solved = split(lanes(w_ref[:, c], u_ref[:, c]))
            v = v_ref[:, c]
            reads, locals_ = [], []
            for h in range(2):
                part = gram[p][h * n : (h + 1) * n]
                both = wide(split(jnp.where(weak, part[:, :n], 0.0)), solved)
                direct = exact_right(split(jnp.where(weak, part[:, n:], 0.0)), v)
                reads.append(both[:, :PAIR])
                locals_.append(both[:, PAIR:] + direct)
            seen = read[p] + jnp.where(low, *reads)
            here = jnp.where(low, *locals_)
            parts = split(seen)
            move, end = other_ref[0, g * GROUP + p], other_ref[1, g * GROUP + p]
            read_ref[:, c] = jnp.where(late, square(parts, split(diagonal_blocks(move))), seen)
            passed = here + square_nt(parts, split(diagonal_blocks(end)))
            local_ref[:, c] = jnp.where(late, passed, here)
            product = q_ref[:, c].astype(F32) * k_ref[:, c].astype(F32) * boost_ref[:, c]
            base_ref[:, c] = head_sum(product, ones) * v.astype(F32) + shift_ref[:, c]
        stores += moved(results, outputs, out_sems, g)
        for copy in stores[-3:]:
            copy.start()
    for copy in stores:
        copy.wait()


def scan_kernel(slots_ref, entry_ref, mask_ref, after_ref, starts_out, exit_ref, starts, sems):
    del after_ref
    count, short = slots_ref.shape[0], starts.shape[1]
    low = low_half(short)
    mask = mask_ref[...]
    state = entry_ref[...]
    chunk = count // sems.shape[0]
    stores = []
    for d in range(count):
        starts[2 * d] = starts[2 * d + 1] = jnp.where(low, state[:short], state[short:])
        if d % chunk == chunk - 1:
            part = pl.ds(2 * (d + 1 - chunk), 2 * chunk)
            stores.append(pltpu.make_async_copy(starts.at[part], starts_out.at[part], sems.at[d // chunk]))
            stores[-1].start()
        hi, lo = split(slots_ref[d, :CH, :])
        weights = rows(lanes(hi, hi), lanes(hi, hi), lanes(lo, lo), lanes(lo, lo))
        end = slots_ref[d, CH:, :]
        turned = pltpu.roll(end, CH, 1)
        fresh = rows(jnp.where(low, end, turned), jnp.where(low, turned, end))
        out = mxu(lanes(*split(state * mask)), weights, NT)
        state = out[:, :PAIR] + out[:, PAIR:] + fresh
    exit_ref[...] = state
    for copy in stores:
        copy.wait()


def final_kernel(starts_ref, read_in, local_in, base_in, gain_ref, out, *scratch, columns):
    buffers, (begins, result, in_sems, out_sems) = scratch[:3], scratch[3:]
    read_ref, local_ref, base_ref = buffers
    cut = [slice(p * PAIR, (p + 1) * PAIR) for p in range(PAIRS)]
    place = [pl.ds(p * PAIR, PAIR) for p in range(PAIRS)]
    block = GROUP * PAIR
    loads = []
    for g in range(WIDTH // block):
        here = pl.ds(g * block, block)
        for i, (src, dst) in enumerate(zip((read_in, local_in, base_in), buffers)):
            loads.append(pltpu.make_async_copy(src.at[:, here], dst.at[:, here], in_sems.at[g, i]))
    for copy in loads:
        copy.start()
    short = starts_ref.shape[1]
    low = low_half(short)
    for owner in range(starts_ref.shape[0]):
        part = starts_ref[owner]
        turned = pltpu.roll(part, CH, 1)
        at = owner * columns
        begins[at : at + short, :] = jnp.where(low, part, turned)
        begins[at + short : at + columns, :] = jnp.where(low, turned, part)[: columns - short]
    own = (iota((PAIR, PAIR), 0) < CH) == low_half(PAIR)
    ones = block_ones()
    right = [split(jnp.where(own, begins[c, :], 0.0)) for c in cut]
    stores = []
    for g in range(PAIRS // GROUP):
        for copy in loads[3 * g : 3 * g + 3]:
            copy.wait()
        pairs = range(g * GROUP, (g + 1) * GROUP)
        left = [split(read_ref[:, cut[p]]) for p in pairs]
        carried = [
            mxu(lanes(*a), lanes(right[p][0], right[p][0]), NT) + mxu(a[0], right[p][1], NT)
            for p, a in zip(pairs, left)
        ]
        readout = [x + local_ref[:, cut[p]] for p, x in zip(pairs, carried)]
        centred = [x - head_sum(x, ones) * (1.0 / CH) for x in readout]
        variance = [head_sum(x * x, ones) * (1.0 / CH) for x in centred]
        for p, x, y in zip(pairs, centred, variance):
            scaled = x * lax.rsqrt(y + 1e-05) * gain_ref[:, cut[p]]
            result[:, cut[p]] = (scaled + base_ref[:, cut[p]]).astype(BF16)
            stores.append(pltpu.make_async_copy(result.at[:, place[p]], out.at[:, place[p]], out_sems.at[p]))
            stores[-1].start()
    for copy in stores:
        copy.wait()


def call(kernel, **kwargs):
    params = pltpu.CompilerParams(vmem_limit_bytes=48 * 1024 * 1024)
    return pl.pallas_call(kernel, interpret=INTERPRET, compiler_params=params, **kwargs)


def shards(q, k, v, raw, rates, logs, memory, boost, gain, shift):
    n = q.shape[0]
    owners = lax.axis_size("ctx")
    columns = memory.shape[1]
    short = (columns + 15) // 16 * 8
    groups = PAIRS // GROUP
    hbm = pl.BlockSpec(memory_space=pltpu.HBM)
    vmem = pl.BlockSpec(memory_space=pltpu.VMEM)
    plane = jax.ShapeDtypeStruct((n, WIDTH), F32)
    tokens = pltpu.VMEM((n, WIDTH), BF16)
    floats = pltpu.VMEM((n, WIDTH), F32)
    sems = pltpu.SemaphoreType.DMA

    pieces = (2, PAIRS, CH, PAIR)
    mine, w, u = call(
        local_kernel,
        in_specs=[hbm] * 5,
        out_specs=[hbm] * 3,
        out_shape=[jax.ShapeDtypeStruct(pieces, F32), plane, plane],
        scratch_shapes=[tokens] * 5
        + [pltpu.VMEM(pieces, F32), floats, floats, sems((groups, 5)), sems((groups, 3))],
    )(k, v, raw, rates, logs)
    other = lax.ppermute(mine, "ctx", [(i, i ^ 1) for i in range(owners)])
    place = lax.axis_index("ctx")
    late = jnp.broadcast_to((place % 2).astype(F32), (1, PAIR))
    slots = call(
        functools.partial(compose_kernel, columns=columns),
        out_shape=jax.ShapeDtypeStruct((owners // 2, CH + short, PAIR), F32),
        scratch_shapes=[pltpu.VMEM((PAIRS, CH, PAIR), F32), pltpu.VMEM((WIDTH, PAIR), F32)],
    )(mine, other, late)
    same_core = [list(range(core, owners, 2)) for core in range(2)]
    slots = lax.all_to_all(slots, "ctx", 0, 0, axis_index_groups=same_core)

    read, local, base = call(
        read_kernel,
        in_specs=[hbm] * 8 + [vmem] * 4,
        out_specs=[hbm] * 3,
        out_shape=[plane] * 3,
        scratch_shapes=[tokens] * 6 + [floats] * 5 + [sems((groups, 8)), sems((groups, 3))],
    )(q, k, v, raw, rates, logs, w, u, boost.reshape(1, WIDTH), shift.reshape(1, WIDTH), other, late)

    own = lax.broadcasted_iota(jnp.int32, (2 * short, PAIR), 0)
    half = lax.broadcasted_iota(jnp.int32, (2 * short, PAIR), 1) // CH
    mask = ((place * columns + own) // CH % 2 == half) & (own < columns)
    entry = jnp.pad(memory.T, ((0, 2 * short - columns), (0, 0)))
    starts, final = call(
        scan_kernel,
        in_specs=[vmem, vmem, vmem, hbm],
        out_specs=[hbm, vmem],
        out_shape=[
            jax.ShapeDtypeStruct((owners, short, PAIR), F32),
            jax.ShapeDtypeStruct((2 * short, PAIR), F32),
        ],
        scratch_shapes=[pltpu.VMEM((owners, short, PAIR), F32), sems((4,))],
    )(slots, jnp.concatenate([entry, entry], axis=1), mask.astype(F32), base)
    starts = lax.all_to_all(starts, "ctx", 0, 0)
    exit_state = final[:columns, :CH].T

    out = call(
        functools.partial(final_kernel, columns=columns),
        in_specs=[vmem, hbm, hbm, hbm, vmem],
        out_specs=hbm,
        out_shape=jax.ShapeDtypeStruct((n, WIDTH), BF16),
        scratch_shapes=[floats] * 3
        + [pltpu.VMEM((WIDTH, PAIR), F32), tokens, sems((groups, 3)), sems((PAIRS,))],
    )(starts, read, local, base, gain.reshape(1, WIDTH))
    return out, exit_state


def solution(mesh):
    rows_spec = P(("dp", "ctx"), None)
    return jax.shard_map(
        shards,
        mesh=mesh,
        in_specs=(rows_spec,) * 6 + (P("dp", "ctx"), P(), P(), P()),
        out_specs=(rows_spec, P("dp", "ctx")),
        check_vma=False,
    )
```

```python
import functools

import jax
import jax.numpy as jnp
from jax import lax
from jax.experimental import pallas as pl
from jax.experimental.pallas import tpu as pltpu
from jax.sharding import PartitionSpec as P

HEADS = 20
CH = 64
PAIR = 2 * CH
PAIRS = HEADS // 2
WIDTH = HEADS * CH
GROUP = 5
INTERPRET = False
F32 = jnp.float32
BF16 = jnp.bfloat16
NN = (((1,), (0,)), ((), ()))
NT = (((1,), (1,)), ((), ()))


def mxu(a, b, dims=NN):
    return lax.dot_general(a, b, dims, preferred_element_type=F32)


def split(x):
    hi = x.astype(BF16)
    return hi, (x - hi.astype(F32)).astype(BF16)


def lanes(*xs):
    return jnp.concatenate(xs, axis=1)


def rows(*xs):
    return jnp.concatenate(xs, axis=0)


def square(a, b):
    both = lanes(*b)
    out = mxu(lanes(*a), rows(both, both))
    return out[:, :PAIR] + out[:, PAIR:]


def stacked(a, b):
    n = a[0].shape[0]
    out = mxu(rows(*a), lanes(*b))
    return out[:n, :PAIR] + out[:n, PAIR:] + out[n:, :PAIR]


def wide(a, b):
    return mxu(lanes(*a), rows(b[0], b[0])) + mxu(a[0], b[1])


def exact_right(a, b):
    return mxu(lanes(*a), rows(b, b))


def iota(shape, dim):
    return lax.broadcasted_iota(jnp.int32, shape, dim)


def low_half(n):
    return iota((n, PAIR), 1) < CH


def block_ones():
    same = (iota((PAIR, PAIR), 0) < CH) == (iota((PAIR, PAIR), 1) < CH)
    return jnp.where(same, 1.0, 0.0).astype(BF16)


def head_sum(x, ones):
    return exact_right(split(x), ones)


def decays(logs, tril):
    return mxu(tril, logs)


def units(raw, ones):
    raw = raw.astype(F32)
    return raw * lax.rsqrt(head_sum(raw * raw, ones) + CH * 1e-05)


def tril_ones(n):
    return jnp.where(iota((n, n), 0) >= iota((n, n), 1), 1.0, 0.0).astype(BF16)


def grams(left, right, low):
    zero = jnp.zeros_like(left)
    stacked = split(rows(jnp.where(low, left, zero), jnp.where(low, zero, left)))
    b = split(right)
    return mxu(lanes(*stacked), lanes(b[0], b[0]), NT) + mxu(stacked[0], b[1], NT)


def inverse(inner):
    n = inner[0].shape[0]
    slab = 16
    count = n // slab
    row, lane = iota((slab, n), 0), iota((slab, n), 1)
    apart = row ^ (lane % slab)
    same = jnp.where(iota((n, n), 0) // slab == iota((n, n), 1) // slab, 1.0, 0.0)
    same_short = same.astype(BF16)

    def spread(pair):
        return tuple(rows(*[x] * count) * same_short for x in pair)

    small = [sum(jnp.where(lane // slab == i, x[i * slab : (i + 1) * slab], 0.0) for i in range(count)) for x in inner]
    solver = [jnp.where(apart == 0, 1.0, 0.0) + jnp.where(apart == 1, x, 0.0) for x in small]
    size = 2
    while size < slab:
        joins = (apart >= size) & (apart < 2 * size)
        halves = [split(x) for x in solver]
        mid = [stacked(split(jnp.where(joins, x, 0.0)), spread(t)) for x, t in zip(small, halves)]
        solver = [x + stacked(t, spread(split(m))) for x, t, m in zip(solver, halves, mid)]
        size *= 2
    halves = [spread(split(x)) for x in solver]
    solver = [rows(*[x] * count) * same for x in solver]

    while size < n:
        odd = lambda x: rows(*[x[i : i + size] for i in range(size, n, 2 * size)])

        def joined(even_of, new):
            parts = []
            for i in range(0, n // 2, size):
                parts += [even_of(2 * i), new[i : i + size]]
            return rows(*parts)

        apart = odd(iota((n, n), 0) ^ iota((n, n), 1))
        joins = (apart >= size) & (apart < 2 * size)
        gap = jnp.zeros((size, n), BF16)
        mid = [stacked(split(jnp.where(joins, odd(x), 0.0)), t) for x, t in zip(inner, halves)]
        mid = [tuple(joined(lambda i: gap, m) for m in split(x)) for x in mid]
        later = [
            odd(x) + stacked((odd(t[0]), odd(t[1])), m) for x, t, m in zip(solver, halves, mid)
        ]
        halves = [
            tuple(joined(lambda i: old[i : i + size], new) for old, new in zip(t, split(x)))
            for x, t in zip(later, halves)
        ]
        solver = [joined(lambda i: x[i : i + size], y) for x, y in zip(solver, later)]
        size *= 2
    return halves


def local_kernel(*refs):
    inputs, (pieces_out, w_out, u_out) = refs[:5], refs[5:8]
    buffers = refs[8:13]
    pieces, w_all, u_all, in_sems, out_sems = refs[13:]
    n, width = w_all.shape
    block = GROUP * PAIR
    groups = width // block
    loads = [
        [
            pltpu.make_async_copy(src.at[:, pl.ds(g * block, block)], dst.at[:, pl.ds(g * block, block)], in_sems.at[g, i])
            for i, (src, dst) in enumerate(zip(inputs, buffers))
        ]
        for g in range(groups)
    ]
    for group in loads:
        for copy in group:
            copy.start()
    k_ref, v_ref, raw_ref, rate_ref, log_ref = buffers
    low = low_half(n)
    ones = block_ones()
    tril = tril_ones(n)
    strict = iota((n, n), 0) > iota((n, n), 1)
    row, lane = iota((CH, PAIR), 0), iota((CH, PAIR), 1)
    stores = []
    pairs = range(GROUP)
    heads = range(2 * GROUP)
    for g in range(groups):
        for copy in loads[g]:
            copy.wait()
        cut = [slice(g * block + p * PAIR, g * block + (p + 1) * PAIR) for p in pairs]
        cumul = [decays(log_ref[:, c], tril) for c in cut]
        unit = [units(raw_ref[:, c], ones) for c in cut]
        alpha = [-unit[p] * jnp.exp(cumul[p] - log_ref[:, cut[p]].astype(F32)) for p in pairs]
        fall = [jnp.exp(-cumul[p]) for p in pairs]
        beta = [rate_ref[:, cut[p]].astype(F32) * unit[p] * fall[p] for p in pairs]
        key = [k_ref[:, cut[p]].astype(F32) * fall[p] for p in pairs]
        gram = [grams(alpha[p], rows(beta[p], key[p]), low) for p in pairs]

        inner, cross = [], []
        for h in heads:
            part = gram[h // 2][(h % 2) * n : (h % 2 + 1) * n]
            inner.append(jnp.where(strict, part[:, :n], 0.0))
            cross.append(jnp.where(strict, part[:, n:], 0.0))
        akv = [exact_right(split(cross[h]), v_ref[:, cut[h // 2]]) for h in heads]
        akv = [jnp.where(low, akv[2 * p], akv[2 * p + 1]) for p in pairs]
        right = [split(lanes(alpha[p], akv[p])) for p in pairs]
        solver = inverse(inner)
        solved = [wide(solver[h], right[h // 2]) for h in heads]
        for p in pairs:
            first, second = solved[2 * p], solved[2 * p + 1]
            w = jnp.where(low, first[:, :PAIR], second[:, :PAIR])
            u = jnp.where(low, first[:, PAIR:], second[:, PAIR:])
            w_all[:, cut[p]] = w
            u_all[:, cut[p]] = u
            scale = jnp.exp(cumul[p][n - 1 :, :])
            end_b = beta[p] * scale
            end_k = key[p] * scale
            moved = square(split(end_b.T), split(w))
            diagonal = jnp.where(row == lane % CH, scale, 0.0)
            pieces[0, g * GROUP + p] = jnp.where(low_half(CH), moved[:CH], moved[CH:]) + diagonal
            content = v_ref[:, cut[p]].astype(F32).T.astype(BF16)
            by_key = mxu(content, lanes(*split(end_k)))
            fresh = square(split(u.T), split(end_b)) + by_key[:, :PAIR] + by_key[:, PAIR:]
            pieces[1, g * GROUP + p] = jnp.where(low_half(CH), fresh[:CH], fresh[CH:])

        here = pl.ds(g * block, block)
        ready = pl.ds(g * GROUP, GROUP)
        stores += [
            pltpu.make_async_copy(pieces.at[:, ready], pieces_out.at[:, ready], out_sems.at[g, 0]),
            pltpu.make_async_copy(w_all.at[:, here], w_out.at[:, here], out_sems.at[g, 1]),
            pltpu.make_async_copy(u_all.at[:, here], u_out.at[:, here], out_sems.at[g, 2]),
        ]
        for copy in stores[-3:]:
            copy.start()
    for copy in stores:
        copy.wait()


def diagonal_blocks(x):
    own = (iota((PAIR, PAIR), 0) < CH) == low_half(PAIR)
    return jnp.where(own, rows(x, x), 0.0)


def square_nt(a, b):
    out = mxu(lanes(*a), rows(lanes(b[0], b[0]), lanes(b[1], b[1])), NT)
    return out[:, :PAIR] + out[:, PAIR:]


def compose_kernel(mine_ref, other_ref, late_ref, slots_ref, moves, ends, *, columns):
    late = late_ref[...] > 0.5
    low = low_half(CH)
    short = (columns + 15) // 16 * 8
    for p in range(PAIRS):
        mine, other = mine_ref[0, p], other_ref[0, p]
        first, second = jnp.where(late, other, mine), jnp.where(late, mine, other)
        moves[p] = square(split(second), split(diagonal_blocks(first)))
        mine, other = mine_ref[1, p], other_ref[1, p]
        first, end = jnp.where(late, other, mine), jnp.where(late, mine, other)
        end = end + square_nt(split(first), split(diagonal_blocks(second)))
        turned = pltpu.roll(end, CH, 1)
        ends[p * PAIR : p * PAIR + CH, :] = jnp.where(low, end, turned)
        ends[p * PAIR + CH : (p + 1) * PAIR, :] = jnp.where(low, turned, end)

    def packed(owner):
        at = owner * columns
        first, last = at // CH, (at + columns - 1) // CH
        slot = moves[first // 2]
        if first // 2 != last // 2:
            slot = jnp.where(low, moves[last // 2], slot)
        tail = rows(ends[at + short : at + columns, :], jnp.zeros((2 * short - columns, PAIR), F32))
        return slot, jnp.where(low_half(short), ends[at : at + short, :], tail)

    for chip in range(slots_ref.shape[0]):
        (move_a, end_a), (move_b, end_b) = packed(2 * chip), packed(2 * chip + 1)
        slots_ref[chip, :CH, :] = jnp.where(late, move_b, move_a)
        slots_ref[chip, CH:, :] = jnp.where(late, end_b, end_a)


def read_kernel(*refs):
    inputs, (boost_ref, shift_ref, other_ref, late_ref) = refs[:8], refs[8:12]
    outputs = refs[12:15]
    buffers = refs[15:23]
    results, in_sems, out_sems = refs[23:26], refs[26], refs[27]
    n, width = results[0].shape
    block = GROUP * PAIR
    groups = width // block

    def moved(sources, targets, sems, g):
        here = pl.ds(g * block, block)
        return [
            pltpu.make_async_copy(src.at[:, here], dst.at[:, here], sems.at[g, i])
            for i, (src, dst) in enumerate(zip(sources, targets))
        ]

    loads = [moved(inputs, buffers, in_sems, g) for g in range(groups)]
    for group in loads:
        for copy in group:
            copy.start()
    q_ref, k_ref, v_ref, raw_ref, rate_ref, log_ref, w_ref, u_ref = buffers
    read_ref, local_ref, base_ref = results
    low = low_half(n)
    ones = block_ones()
    tril = tril_ones(n)
    weak = iota((n, n), 0) >= iota((n, n), 1)
    late = late_ref[...] > 0.5
    pairs = range(GROUP)
    stores = []
    for g in range(groups):
        for copy in loads[g]:
            copy.wait()
        cut = [slice(g * block + p * PAIR, g * block + (p + 1) * PAIR) for p in pairs]
        cumul = [decays(log_ref[:, c], tril) for c in cut]
        unit = [units(raw_ref[:, c], ones) for c in cut]
        fall = [jnp.exp(-cumul[p]) for p in pairs]
        beta = [rate_ref[:, cut[p]].astype(F32) * unit[p] * fall[p] for p in pairs]
        key = [k_ref[:, cut[p]].astype(F32) * fall[p] for p in pairs]
        read = [q_ref[:, cut[p]].astype(F32) * jnp.exp(cumul[p]) for p in pairs]
        gram = [grams(read[p], rows(beta[p], key[p]), low) for p in pairs]
        for p in pairs:
            c = cut[p]
            solved = split(lanes(w_ref[:, c], u_ref[:, c]))
            v = v_ref[:, c]
            reads, locals_ = [], []
            for h in range(2):
                part = gram[p][h * n : (h + 1) * n]
                both = wide(split(jnp.where(weak, part[:, :n], 0.0)), solved)
                direct = exact_right(split(jnp.where(weak, part[:, n:], 0.0)), v)
                reads.append(both[:, :PAIR])
                locals_.append(both[:, PAIR:] + direct)
            seen = read[p] + jnp.where(low, *reads)
            here = jnp.where(low, *locals_)
            parts = split(seen)
            move, end = other_ref[0, g * GROUP + p], other_ref[1, g * GROUP + p]
            read_ref[:, c] = jnp.where(late, square(parts, split(diagonal_blocks(move))), seen)
            passed = here + square_nt(parts, split(diagonal_blocks(end)))
            local_ref[:, c] = jnp.where(late, passed, here)
            product = q_ref[:, c].astype(F32) * k_ref[:, c].astype(F32) * boost_ref[:, c]
            base_ref[:, c] = head_sum(product, ones) * v.astype(F32) + shift_ref[:, c]
        stores += moved(results, outputs, out_sems, g)
        for copy in stores[-3:]:
            copy.start()
    for copy in stores:
        copy.wait()


def scan_kernel(slots_ref, entry_ref, mask_ref, after_ref, starts_out, exit_ref, starts, sems):
    del after_ref
    count, short = slots_ref.shape[0], starts.shape[1]
    low = low_half(short)
    mask = mask_ref[...]
    state = entry_ref[...]
    chunk = count // sems.shape[0]
    stores = []
    for d in range(count):
        starts[2 * d] = starts[2 * d + 1] = jnp.where(low, state[:short], state[short:])
        if d % chunk == chunk - 1:
            part = pl.ds(2 * (d + 1 - chunk), 2 * chunk)
            stores.append(pltpu.make_async_copy(starts.at[part], starts_out.at[part], sems.at[d // chunk]))
            stores[-1].start()
        hi, lo = split(slots_ref[d, :CH, :])
        weights = rows(lanes(hi, hi), lanes(hi, hi), lanes(lo, lo), lanes(lo, lo))
        end = slots_ref[d, CH:, :]
        turned = pltpu.roll(end, CH, 1)
        fresh = rows(jnp.where(low, end, turned), jnp.where(low, turned, end))
        out = mxu(lanes(*split(state * mask)), weights, NT)
        state = out[:, :PAIR] + out[:, PAIR:] + fresh
    exit_ref[...] = state
    for copy in stores:
        copy.wait()


def final_kernel(starts_ref, read_in, local_in, base_in, gain_ref, out, *scratch, columns):
    buffers, (begins, result, in_sems, out_sems) = scratch[:3], scratch[3:]
    read_ref, local_ref, base_ref = buffers
    cut = [slice(p * PAIR, (p + 1) * PAIR) for p in range(PAIRS)]
    place = [pl.ds(p * PAIR, PAIR) for p in range(PAIRS)]
    block = GROUP * PAIR
    loads = []
    for g in range(WIDTH // block):
        here = pl.ds(g * block, block)
        for i, (src, dst) in enumerate(zip((read_in, local_in, base_in), buffers)):
            loads.append(pltpu.make_async_copy(src.at[:, here], dst.at[:, here], in_sems.at[g, i]))
    for copy in loads:
        copy.start()
    short = starts_ref.shape[1]
    low = low_half(short)
    for owner in range(starts_ref.shape[0]):
        part = starts_ref[owner]
        turned = pltpu.roll(part, CH, 1)
        at = owner * columns
        begins[at : at + short, :] = jnp.where(low, part, turned)
        begins[at + short : at + columns, :] = jnp.where(low, turned, part)[: columns - short]
    own = (iota((PAIR, PAIR), 0) < CH) == low_half(PAIR)
    ones = block_ones()
    right = [split(jnp.where(own, begins[c, :], 0.0)) for c in cut]
    stores = []
    for g in range(PAIRS // GROUP):
        for copy in loads[3 * g : 3 * g + 3]:
            copy.wait()
        pairs = range(g * GROUP, (g + 1) * GROUP)
        left = [split(read_ref[:, cut[p]]) for p in pairs]
        carried = [
            mxu(lanes(*a), lanes(right[p][0], right[p][0]), NT) + mxu(a[0], right[p][1], NT)
            for p, a in zip(pairs, left)
        ]
        readout = [x + local_ref[:, cut[p]] for p, x in zip(pairs, carried)]
        centred = [x - head_sum(x, ones) * (1.0 / CH) for x in readout]
        variance = [head_sum(x * x, ones) * (1.0 / CH) for x in centred]
        for p, x, y in zip(pairs, centred, variance):
            scaled = x * lax.rsqrt(y + 1e-05) * gain_ref[:, cut[p]]
            result[:, cut[p]] = (scaled + base_ref[:, cut[p]]).astype(BF16)
            stores.append(pltpu.make_async_copy(result.at[:, place[p]], out.at[:, place[p]], out_sems.at[p]))
            stores[-1].start()
    for copy in stores:
        copy.wait()


def call(kernel, **kwargs):
    params = pltpu.CompilerParams(vmem_limit_bytes=48 * 1024 * 1024)
    return pl.pallas_call(kernel, interpret=INTERPRET, compiler_params=params, **kwargs)


def shards(q, k, v, raw, rates, logs, memory, boost, gain, shift):
    n = q.shape[0]
    owners = lax.axis_size("ctx")
    columns = memory.shape[1]
    short = (columns + 15) // 16 * 8
    groups = PAIRS // GROUP
    hbm = pl.BlockSpec(memory_space=pltpu.HBM)
    held = functools.partial(pltpu.with_memory_space_constraint, memory_space=pltpu.HBM)
    vmem = pl.BlockSpec(memory_space=pltpu.VMEM)
    plane = pltpu.HBM((n, WIDTH), F32)
    arrays = [held(x) for x in (q, k, v, raw, rates, logs)]
    tokens = pltpu.VMEM((n, WIDTH), BF16)
    floats = pltpu.VMEM((n, WIDTH), F32)
    sems = pltpu.SemaphoreType.DMA

    pieces = (2, PAIRS, CH, PAIR)
    mine, w, u = call(
        local_kernel,
        in_specs=[hbm] * 5,
        out_specs=[hbm] * 3,
        out_shape=[jax.ShapeDtypeStruct(pieces, F32), plane, plane],
        scratch_shapes=[tokens] * 5
        + [pltpu.VMEM(pieces, F32), floats, floats, sems((groups, 5)), sems((groups, 3))],
    )(*arrays[1:])
    other = lax.ppermute(mine, "ctx", [(i, i ^ 1) for i in range(owners)])
    place = lax.axis_index("ctx")
    late = jnp.broadcast_to((place % 2).astype(F32), (1, PAIR))
    slots = call(
        functools.partial(compose_kernel, columns=columns),
        out_shape=jax.ShapeDtypeStruct((owners // 2, CH + short, PAIR), F32),
        scratch_shapes=[pltpu.VMEM((PAIRS, CH, PAIR), F32), pltpu.VMEM((WIDTH, PAIR), F32)],
    )(mine, other, late)
    same_core = [list(range(core, owners, 2)) for core in range(2)]
    slots = lax.all_to_all(slots, "ctx", 0, 0, axis_index_groups=same_core)

    read, local, base = call(
        read_kernel,
        in_specs=[hbm] * 8 + [vmem] * 4,
        out_specs=[hbm] * 3,
        out_shape=[plane] * 3,
        scratch_shapes=[tokens] * 6 + [floats] * 5 + [sems((groups, 8)), sems((groups, 3))],
    )(*arrays, held(w), held(u), boost.reshape(1, WIDTH), shift.reshape(1, WIDTH), other, late)

    own = lax.broadcasted_iota(jnp.int32, (2 * short, PAIR), 0)
    half = lax.broadcasted_iota(jnp.int32, (2 * short, PAIR), 1) // CH
    mask = ((place * columns + own) // CH % 2 == half) & (own < columns)
    entry = jnp.pad(memory.T, ((0, 2 * short - columns), (0, 0)))
    starts, final = call(
        scan_kernel,
        in_specs=[vmem, vmem, vmem, hbm],
        out_specs=[hbm, vmem],
        out_shape=[
            pltpu.HBM((owners, short, PAIR), F32),
            jax.ShapeDtypeStruct((2 * short, PAIR), F32),
        ],
        scratch_shapes=[pltpu.VMEM((owners, short, PAIR), F32), sems((4,))],
    )(slots, jnp.concatenate([entry, entry], axis=1), mask.astype(F32), held(base))
    starts = lax.all_to_all(starts, "ctx", 0, 0)
    exit_state = final[:columns, :CH].T

    out = call(
        functools.partial(final_kernel, columns=columns),
        in_specs=[vmem, hbm, hbm, hbm, vmem],
        out_specs=hbm,
        out_shape=pltpu.HBM((n, WIDTH), BF16),
        scratch_shapes=[floats] * 3
        + [pltpu.VMEM((WIDTH, PAIR), F32), tokens, sems((groups, 3)), sems((PAIRS,))],
    )(starts, held(read), held(local), held(base), gain.reshape(1, WIDTH))
    return out, exit_state


def solution(mesh):
    rows_spec = P(("dp", "ctx"), None)
    return jax.shard_map(
        shards,
        mesh=mesh,
        in_specs=(rows_spec,) * 6 + (P("dp", "ctx"), P(), P(), P()),
        out_specs=(rows_spec, P("dp", "ctx")),
        check_vma=False,
    )
```

```python
import functools

import jax
import jax.numpy as jnp
from jax import lax
from jax.experimental import pallas as pl
from jax.experimental.pallas import tpu as pltpu
from jax.sharding import PartitionSpec as P

HEADS = 20
CH = 64
PAIR = 2 * CH
PAIRS = HEADS // 2
WIDTH = HEADS * CH
GROUP = 5
INTERPRET = False
F32 = jnp.float32
BF16 = jnp.bfloat16
NN = (((1,), (0,)), ((), ()))
NT = (((1,), (1,)), ((), ()))


def mxu(a, b, dims=NN):
    return lax.dot_general(a, b, dims, preferred_element_type=F32)


def split(x):
    hi = x.astype(BF16)
    return hi, (x - hi.astype(F32)).astype(BF16)


def lanes(*xs):
    return jnp.concatenate(xs, axis=1)


def rows(*xs):
    return jnp.concatenate(xs, axis=0)


def square(a, b):
    both = lanes(*b)
    out = mxu(lanes(*a), rows(both, both))
    return out[:, :PAIR] + out[:, PAIR:]


def wide(a, b):
    return mxu(lanes(*a), rows(b[0], b[0])) + mxu(a[0], b[1])


def exact_right(a, b):
    return mxu(lanes(*a), rows(b, b))


def iota(shape, dim):
    return lax.broadcasted_iota(jnp.int32, shape, dim)


def low_half(n):
    return iota((n, PAIR), 1) < CH


def block_ones():
    same = (iota((PAIR, PAIR), 0) < CH) == (iota((PAIR, PAIR), 1) < CH)
    return jnp.where(same, 1.0, 0.0).astype(BF16)


def head_sum(x, ones):
    return exact_right(split(x), ones)


def decays(logs, tril):
    return mxu(tril, logs)


def units(raw, ones):
    raw = raw.astype(F32)
    return raw * lax.rsqrt(head_sum(raw * raw, ones) + CH * 1e-05)


def tril_ones(n):
    return jnp.where(iota((n, n), 0) >= iota((n, n), 1), 1.0, 0.0).astype(BF16)


def grams(left, right, low):
    zero = jnp.zeros_like(left)
    stacked = split(rows(jnp.where(low, left, zero), jnp.where(low, zero, left)))
    b = split(right)
    return mxu(lanes(*stacked), lanes(b[0], b[0]), NT) + mxu(stacked[0], b[1], NT)


def inverse(inner):
    n = inner[0].shape[0]
    slab = 16
    count = n // slab
    row, lane = iota((slab, n), 0), iota((slab, n), 1)
    apart = row ^ (lane % slab)
    same = jnp.where(iota((n, n), 0) // slab == iota((n, n), 1) // slab, 1.0, 0.0)
    same_short = same.astype(BF16)

    def spread(pair):
        return tuple(rows(*[x] * count) * same_short for x in pair)

    small = [sum(jnp.where(lane // slab == i, x[i * slab : (i + 1) * slab], 0.0) for i in range(count)) for x in inner]
    solver = [jnp.where(apart == 0, 1.0, 0.0) + jnp.where(apart == 1, x, 0.0) for x in small]
    size = 2
    while size < slab:
        joins = (apart >= size) & (apart < 2 * size)
        halves = [split(x) for x in solver]
        mid = [square(split(jnp.where(joins, x, 0.0)), spread(t)) for x, t in zip(small, halves)]
        solver = [x + square(t, spread(split(m))) for x, t, m in zip(solver, halves, mid)]
        size *= 2
    halves = [spread(split(x)) for x in solver]
    solver = [rows(*[x] * count) * same for x in solver]

    while size < n:
        odd = lambda x: rows(*[x[i : i + size] for i in range(size, n, 2 * size)])

        def joined(even_of, new):
            parts = []
            for i in range(0, n // 2, size):
                parts += [even_of(2 * i), new[i : i + size]]
            return rows(*parts)

        apart = odd(iota((n, n), 0) ^ iota((n, n), 1))
        joins = (apart >= size) & (apart < 2 * size)
        gap = jnp.zeros((size, n), BF16)
        mid = [square(split(jnp.where(joins, odd(x), 0.0)), t) for x, t in zip(inner, halves)]
        mid = [tuple(joined(lambda i: gap, m) for m in split(x)) for x in mid]
        later = [
            odd(x) + square((odd(t[0]), odd(t[1])), m) for x, t, m in zip(solver, halves, mid)
        ]
        halves = [
            tuple(joined(lambda i: old[i : i + size], new) for old, new in zip(t, split(x)))
            for x, t in zip(later, halves)
        ]
        solver = [joined(lambda i: x[i : i + size], y) for x, y in zip(solver, later)]
        size *= 2
    return halves


def local_kernel(*refs):
    inputs, (pieces_out, w_out, u_out) = refs[:5], refs[5:8]
    buffers = refs[8:13]
    pieces, w_all, u_all, in_sems, out_sems = refs[13:]
    n, width = w_all.shape
    order = (4, 3, 2, 0, 1)
    loads = [pltpu.make_async_copy(inputs[i], buffers[i], in_sems.at[i]) for i in range(5)]
    for i in order:
        loads[i].start()
    k_ref, v_ref, raw_ref, rate_ref, log_ref = buffers
    pairs = range(width // PAIR)
    heads = range(2 * len(pairs))
    cut = [slice(p * PAIR, (p + 1) * PAIR) for p in pairs]
    low = low_half(n)
    ones = block_ones()
    tril = tril_ones(n)
    strict = iota((n, n), 0) > iota((n, n), 1)
    row, lane = iota((CH, PAIR), 0), iota((CH, PAIR), 1)

    loads[4].wait()
    cumul = [decays(log_ref[:, c], tril) for c in cut]
    fall = [jnp.exp(-x) for x in cumul]
    rise = [jnp.exp(x - log_ref[:, c].astype(F32)) for x, c in zip(cumul, cut)]
    loads[2].wait()
    unit = [units(raw_ref[:, c], ones) for c in cut]
    alpha = [-x * y for x, y in zip(unit, rise)]
    loads[3].wait()
    beta = [rate_ref[:, c].astype(F32) * x * y for c, x, y in zip(cut, unit, fall)]
    loads[0].wait()
    key = [k_ref[:, c].astype(F32) * x for c, x in zip(cut, fall)]
    gram = [grams(alpha[p], rows(beta[p], key[p]), low) for p in pairs]
    inner, cross = [], []
    for h in heads:
        part = gram[h // 2][(h % 2) * n : (h % 2 + 1) * n]
        inner.append(jnp.where(strict, part[:, :n], 0.0))
        cross.append(jnp.where(strict, part[:, n:], 0.0))
    loads[1].wait()
    akv = [exact_right(split(cross[h]), v_ref[:, cut[h // 2]]) for h in heads]
    akv = [pltpu.roll(jnp.where(low, akv[2 * p], akv[2 * p + 1]), CH, 1) for p in pairs]
    right = []
    for p in pairs:
        right += [split(jnp.where(low, alpha[p], akv[p])), split(jnp.where(low, akv[p], alpha[p]))]
    solver = inverse(inner)
    solved = [square(solver[h], right[h]) for h in heads]
    w = [jnp.where(low, solved[2 * p], solved[2 * p + 1]) for p in pairs]
    u = [pltpu.roll(jnp.where(low, solved[2 * p + 1], solved[2 * p]), CH, 1) for p in pairs]
    stores = []

    def store(slot, src, dst):
        stores.append(pltpu.make_async_copy(src, dst, out_sems.at[slot]))
        stores[-1].start()

    for p in pairs:
        w_all[:, cut[p]] = w[p]
        u_all[:, cut[p]] = u[p]
        here = pl.ds(p * PAIR, PAIR)
        store(4 * p, w_all.at[:, here], w_out.at[:, here])
        store(4 * p + 1, u_all.at[:, here], u_out.at[:, here])
    scale = [jnp.exp(x[n - 1 :, :]) for x in cumul]
    end_b = [x * y for x, y in zip(beta, scale)]
    moved = [square(split(x.T), split(y)) for x, y in zip(end_b, w)]
    for p in pairs:
        diagonal = jnp.where(row == lane % CH, scale[p], 0.0)
        pieces[0, p] = jnp.where(low_half(CH), moved[p][:CH], moved[p][CH:]) + diagonal
        store(4 * p + 2, pieces.at[0, p], pieces_out.at[0, p])
    by_key = [
        mxu(v_ref[:, c].astype(F32).T.astype(BF16), lanes(*split(x * y))) for c, x, y in zip(cut, key, scale)
    ]
    fresh = [square(split(x.T), split(y)) for x, y in zip(u, end_b)]
    for p in pairs:
        end = fresh[p] + by_key[p][:, :PAIR] + by_key[p][:, PAIR:]
        pieces[1, p] = jnp.where(low_half(CH), end[:CH], end[CH:])
        store(4 * p + 3, pieces.at[1, p], pieces_out.at[1, p])
    for copy in stores:
        copy.wait()


def diagonal_blocks(x):
    own = (iota((PAIR, PAIR), 0) < CH) == low_half(PAIR)
    return jnp.where(own, rows(x, x), 0.0)


def square_nt(a, b):
    out = mxu(lanes(*a), rows(lanes(b[0], b[0]), lanes(b[1], b[1])), NT)
    return out[:, :PAIR] + out[:, PAIR:]


def compose_kernel(mine_ref, other_ref, late_ref, slots_ref, moves, ends, *, columns):
    late = late_ref[...] > 0.5
    low = low_half(CH)
    short = (columns + 15) // 16 * 8
    pairs = range(PAIRS)
    first = [jnp.where(late, other_ref[0, p], mine_ref[0, p]) for p in pairs]
    second = [jnp.where(late, mine_ref[0, p], other_ref[0, p]) for p in pairs]
    moved = [square(split(y), split(diagonal_blocks(x))) for x, y in zip(first, second)]
    first = [jnp.where(late, other_ref[1, p], mine_ref[1, p]) for p in pairs]
    carried = [square_nt(split(x), split(diagonal_blocks(y))) for x, y in zip(first, second)]
    for p in pairs:
        moves[p] = moved[p]
        end = carried[p] + jnp.where(late, mine_ref[1, p], other_ref[1, p])
        turned = pltpu.roll(end, CH, 1)
        ends[p * PAIR : p * PAIR + CH, :] = jnp.where(low, end, turned)
        ends[p * PAIR + CH : (p + 1) * PAIR, :] = jnp.where(low, turned, end)

    def packed(owner):
        at = owner * columns
        first, last = at // CH, (at + columns - 1) // CH
        slot = moves[first // 2]
        if first // 2 != last // 2:
            slot = jnp.where(low, moves[last // 2], slot)
        tail = rows(ends[at + short : at + columns, :], jnp.zeros((2 * short - columns, PAIR), F32))
        return slot, jnp.where(low_half(short), ends[at : at + short, :], tail)

    for chip in range(slots_ref.shape[0]):
        (move_a, end_a), (move_b, end_b) = packed(2 * chip), packed(2 * chip + 1)
        slots_ref[chip, :CH, :] = jnp.where(late, move_b, move_a)
        slots_ref[chip, CH:, :] = jnp.where(late, end_b, end_a)


def read_kernel(*refs):
    inputs, (boost_ref, shift_ref, other_ref, late_ref) = refs[:8], refs[8:12]
    outputs = refs[12:15]
    buffers = refs[15:23]
    results, in_sems, out_sems = refs[23:26], refs[26], refs[27]
    n, width = results[0].shape
    block = GROUP * PAIR
    groups = width // block

    def moved(sources, targets, sems, g):
        here = pl.ds(g * block, block)
        return [
            pltpu.make_async_copy(src.at[:, here], dst.at[:, here], sems.at[g, i])
            for i, (src, dst) in enumerate(zip(sources, targets))
        ]

    loads = [moved(inputs, buffers, in_sems, g) for g in range(groups)]
    for group in loads:
        for copy in group:
            copy.start()
    q_ref, k_ref, v_ref, raw_ref, rate_ref, log_ref, w_ref, u_ref = buffers
    read_ref, local_ref, base_ref = results
    low = low_half(n)
    ones = block_ones()
    tril = tril_ones(n)
    weak = iota((n, n), 0) >= iota((n, n), 1)
    late = late_ref[...] > 0.5
    pairs = range(GROUP)
    stores = []
    for g in range(groups):
        for copy in loads[g]:
            copy.wait()
        cut = [slice(g * block + p * PAIR, g * block + (p + 1) * PAIR) for p in pairs]
        cumul = [decays(log_ref[:, c], tril) for c in cut]
        unit = [units(raw_ref[:, c], ones) for c in cut]
        fall = [jnp.exp(-cumul[p]) for p in pairs]
        beta = [rate_ref[:, cut[p]].astype(F32) * unit[p] * fall[p] for p in pairs]
        key = [k_ref[:, cut[p]].astype(F32) * fall[p] for p in pairs]
        read = [q_ref[:, cut[p]].astype(F32) * jnp.exp(cumul[p]) for p in pairs]
        gram = [grams(read[p], rows(beta[p], key[p]), low) for p in pairs]
        for p in pairs:
            c = cut[p]
            solved = split(lanes(w_ref[:, c], u_ref[:, c]))
            v = v_ref[:, c]
            reads, locals_ = [], []
            for h in range(2):
                part = gram[p][h * n : (h + 1) * n]
                both = wide(split(jnp.where(weak, part[:, :n], 0.0)), solved)
                direct = exact_right(split(jnp.where(weak, part[:, n:], 0.0)), v)
                reads.append(both[:, :PAIR])
                locals_.append(both[:, PAIR:] + direct)
            seen = read[p] + jnp.where(low, *reads)
            here = jnp.where(low, *locals_)
            parts = split(seen)
            move, end = other_ref[0, g * GROUP + p], other_ref[1, g * GROUP + p]
            read_ref[:, c] = jnp.where(late, square(parts, split(diagonal_blocks(move))), seen)
            passed = here + square_nt(parts, split(diagonal_blocks(end)))
            local_ref[:, c] = jnp.where(late, passed, here)
            product = q_ref[:, c].astype(F32) * k_ref[:, c].astype(F32) * boost_ref[:, c]
            base_ref[:, c] = head_sum(product, ones) * v.astype(F32) + shift_ref[:, c]
        stores += moved(results, outputs, out_sems, g)
        for copy in stores[-3:]:
            copy.start()
    for copy in stores:
        copy.wait()


def scan_kernel(slots_ref, entry_ref, mask_ref, after_ref, starts_out, exit_ref, starts, sems):
    del after_ref
    count, short = slots_ref.shape[0], starts.shape[1]
    low = low_half(short)
    mask = mask_ref[...]

    def weights(move):
        hi, lo = move
        return rows(lanes(hi, hi), lanes(hi, hi), lanes(lo, lo), lanes(lo, lo))

    def advance(state, move, fresh):
        out = mxu(lanes(*split(state * mask)), move, NT)
        return out[:, :PAIR] + out[:, PAIR:] + fresh

    def unpacked(d):
        end = slots_ref[d, CH:, :]
        turned = pltpu.roll(end, CH, 1)
        return rows(jnp.where(low, end, turned), jnp.where(low, turned, end))

    parts = [split(slots_ref[d, :CH, :]) for d in range(count)]
    moves = [weights(x) for x in parts]
    fresh = [unpacked(d) for d in range(count)]
    both = [
        weights(split(square(parts[d + 1], split(diagonal_blocks(slots_ref[d, :CH, :])))))
        for d in range(0, count, 2)
    ]
    joint = [advance(fresh[d], moves[d + 1], fresh[d + 1]) for d in range(0, count, 2)]
    states = [entry_ref[...]]
    for d in range(count // 2):
        states.append(advance(states[d], both[d], joint[d]))
    stores = []
    for d in range(count // 2):
        middle = advance(states[d], moves[2 * d], fresh[2 * d])
        for i, x in enumerate((states[d], middle)):
            at = 4 * d + 2 * i
            starts[at] = starts[at + 1] = jnp.where(low, x[:short], x[short:])
        part = pl.ds(4 * d, 4)
        stores.append(pltpu.make_async_copy(starts.at[part], starts_out.at[part], sems.at[d]))
        stores[-1].start()
    exit_ref[...] = states[-1]
    for copy in stores:
        copy.wait()


def final_kernel(starts_ref, read_ref, local_ref, base_ref, gain_ref, out, begins, result, out_sems, *, columns):
    cut = [slice(p * PAIR, (p + 1) * PAIR) for p in range(PAIRS)]
    place = [pl.ds(p * PAIR, PAIR) for p in range(PAIRS)]
    short = starts_ref.shape[1]
    low = low_half(short)
    for owner in range(starts_ref.shape[0]):
        part = starts_ref[owner]
        turned = pltpu.roll(part, CH, 1)
        at = owner * columns
        begins[at : at + short, :] = jnp.where(low, part, turned)
        begins[at + short : at + columns, :] = jnp.where(low, turned, part)[: columns - short]
    own = (iota((PAIR, PAIR), 0) < CH) == low_half(PAIR)
    ones = block_ones()
    right = [split(jnp.where(own, begins[c, :], 0.0)) for c in cut]
    stores = []
    for g in range(PAIRS // GROUP):
        pairs = range(g * GROUP, (g + 1) * GROUP)
        left = [split(read_ref[:, cut[p]]) for p in pairs]
        carried = [
            mxu(lanes(*a), lanes(right[p][0], right[p][0]), NT) + mxu(a[0], right[p][1], NT)
            for p, a in zip(pairs, left)
        ]
        readout = [x + local_ref[:, cut[p]] for p, x in zip(pairs, carried)]
        centred = [x - head_sum(x, ones) * (1.0 / CH) for x in readout]
        variance = [head_sum(x * x, ones) * (1.0 / CH) for x in centred]
        for p, x, y in zip(pairs, centred, variance):
            scaled = x * lax.rsqrt(y + 1e-05) * gain_ref[:, cut[p]]
            result[:, cut[p]] = (scaled + base_ref[:, cut[p]]).astype(BF16)
            stores.append(pltpu.make_async_copy(result.at[:, place[p]], out.at[:, place[p]], out_sems.at[p]))
            stores[-1].start()
    for copy in stores:
        copy.wait()


def call(kernel, **kwargs):
    params = pltpu.CompilerParams(vmem_limit_bytes=48 * 1024 * 1024)
    return pl.pallas_call(kernel, interpret=INTERPRET, compiler_params=params, **kwargs)


def shards(q, k, v, raw, rates, logs, memory, boost, gain, shift):
    n = q.shape[0]
    owners = lax.axis_size("ctx")
    columns = memory.shape[1]
    short = (columns + 15) // 16 * 8
    groups = PAIRS // GROUP
    hbm = pl.BlockSpec(memory_space=pltpu.HBM)
    held = functools.partial(pltpu.with_memory_space_constraint, memory_space=pltpu.HBM)
    vmem = pl.BlockSpec(memory_space=pltpu.VMEM)
    plane = pltpu.HBM((n, WIDTH), F32)
    arrays = [held(x) for x in (q, k, v, raw, rates, logs)]
    tokens = pltpu.VMEM((n, WIDTH), BF16)
    floats = pltpu.VMEM((n, WIDTH), F32)
    sems = pltpu.SemaphoreType.DMA

    pieces = (2, PAIRS, CH, PAIR)
    mine, w, u = call(
        local_kernel,
        in_specs=[hbm] * 5,
        out_specs=[hbm] * 3,
        out_shape=[jax.ShapeDtypeStruct(pieces, F32), plane, plane],
        scratch_shapes=[tokens] * 5
        + [pltpu.VMEM(pieces, F32), floats, floats, sems((5,)), sems((4 * PAIRS,))],
    )(*arrays[1:])
    other = lax.ppermute(mine, "ctx", [(i, i ^ 1) for i in range(owners)])
    place = lax.axis_index("ctx")
    late = jnp.broadcast_to((place % 2).astype(F32), (1, PAIR))
    slots = call(
        functools.partial(compose_kernel, columns=columns),
        out_shape=jax.ShapeDtypeStruct((owners // 2, CH + short, PAIR), F32),
        scratch_shapes=[pltpu.VMEM((PAIRS, CH, PAIR), F32), pltpu.VMEM((WIDTH, PAIR), F32)],
    )(mine, other, late)
    same_core = [list(range(core, owners, 2)) for core in range(2)]
    slots = lax.all_to_all(slots, "ctx", 0, 0, axis_index_groups=same_core)

    read, local, base = call(
        read_kernel,
        in_specs=[hbm] * 8 + [vmem] * 4,
        out_specs=[hbm] * 3,
        out_shape=[jax.ShapeDtypeStruct((n, WIDTH), F32)] * 3,
        scratch_shapes=[tokens] * 6 + [floats] * 5 + [sems((groups, 8)), sems((groups, 3))],
    )(*arrays, held(w), held(u), boost.reshape(1, WIDTH), shift.reshape(1, WIDTH), other, late)

    own = lax.broadcasted_iota(jnp.int32, (2 * short, PAIR), 0)
    half = lax.broadcasted_iota(jnp.int32, (2 * short, PAIR), 1) // CH
    mask = ((place * columns + own) // CH % 2 == half) & (own < columns)
    entry = jnp.pad(memory.T, ((0, 2 * short - columns), (0, 0)))
    starts, final = call(
        scan_kernel,
        in_specs=[vmem, vmem, vmem, hbm],
        out_specs=[hbm, vmem],
        out_shape=[
            pltpu.HBM((owners, short, PAIR), F32),
            jax.ShapeDtypeStruct((2 * short, PAIR), F32),
        ],
        scratch_shapes=[pltpu.VMEM((owners, short, PAIR), F32), sems((owners // 4,))],
    )(slots, jnp.concatenate([entry, entry], axis=1), mask.astype(F32), base)
    starts = lax.all_to_all(starts, "ctx", 0, 0)
    exit_state = final[:columns, :CH].T

    out = call(
        functools.partial(final_kernel, columns=columns),
        in_specs=[vmem] * 5,
        out_specs=hbm,
        out_shape=pltpu.HBM((n, WIDTH), BF16),
        scratch_shapes=[pltpu.VMEM((WIDTH, PAIR), F32), tokens, sems((PAIRS,))],
    )(starts, read, local, base, gain.reshape(1, WIDTH))
    return out, exit_state


def solution(mesh):
    rows_spec = P(("dp", "ctx"), None)
    return jax.shard_map(
        shards,
        mesh=mesh,
        in_specs=(rows_spec,) * 6 + (P("dp", "ctx"), P(), P(), P()),
        out_specs=(rows_spec, P("dp", "ctx")),
        check_vma=False,
    )
```

```python
import functools

import jax
import jax.numpy as jnp
from jax import lax
from jax.experimental import pallas as pl
from jax.experimental.pallas import tpu as pltpu
from jax.sharding import PartitionSpec as P

HEADS = 20
CH = 64
PAIR = 2 * CH
PAIRS = HEADS // 2
WIDTH = HEADS * CH
GROUP = 5
INTERPRET = False
F32 = jnp.float32
BF16 = jnp.bfloat16
NN = (((1,), (0,)), ((), ()))
NT = (((1,), (1,)), ((), ()))


def mxu(a, b, dims=NN):
    return lax.dot_general(a, b, dims, preferred_element_type=F32)


def split(x):
    hi = x.astype(BF16)
    return hi, (x - hi.astype(F32)).astype(BF16)


def lanes(*xs):
    return jnp.concatenate(xs, axis=1)


def rows(*xs):
    return jnp.concatenate(xs, axis=0)


def square(a, b):
    both = lanes(*b)
    out = mxu(lanes(*a), rows(both, both))
    return out[:, :PAIR] + out[:, PAIR:]


def wide(a, b):
    return mxu(lanes(*a), rows(b[0], b[0])) + mxu(a[0], b[1])


def exact_right(a, b):
    return mxu(lanes(*a), rows(b, b))


def iota(shape, dim):
    return lax.broadcasted_iota(jnp.int32, shape, dim)


def low_half(n):
    return iota((n, PAIR), 1) < CH


def block_ones():
    same = (iota((PAIR, PAIR), 0) < CH) == (iota((PAIR, PAIR), 1) < CH)
    return jnp.where(same, 1.0, 0.0).astype(BF16)


def head_sum(x, ones):
    return exact_right(split(x), ones)


def decays(logs, tril):
    return mxu(tril, logs)


def units(raw, ones):
    raw = raw.astype(F32)
    return raw * lax.rsqrt(head_sum(raw * raw, ones) + CH * 1e-05)


def tril_ones(n):
    return jnp.where(iota((n, n), 0) >= iota((n, n), 1), 1.0, 0.0).astype(BF16)


def grams(left, right, low):
    first = jnp.where(low, 1.0, 0.0).astype(BF16)
    second = jnp.where(low, 0.0, 1.0).astype(BF16)
    hi, lo = (rows(x * first, x * second) for x in split(left))
    b = split(right)
    return mxu(lanes(hi, lo), lanes(b[0], b[0]), NT) + mxu(hi, b[1], NT)


def small_inverse(small):
    slab, n = small[0].shape
    parts = lanes(*split(rows(*small)))
    source, target = iota((n, n), 0), iota((n, n), 1)

    def pick(s):
        return jnp.where(source == target // slab * slab + s, 1.0, 0.0).astype(BF16)

    columns = []
    for s in range(0, slab, 2):
        both = lanes(pick(s), pick(s + 1))
        out = mxu(parts, rows(both, both))
        columns += [out[:, :n], out[:, n:]]
    unit = jnp.where(iota((slab, n), 0) == iota((slab, n), 1) % slab, 1.0, 0.0)
    solver = [unit] * len(small)
    for s in range(slab - 1):
        solver = [
            x + columns[s][h * slab : (h + 1) * slab] * x[s : s + 1, :] for h, x in enumerate(solver)
        ]
    return solver


def inverse(inner):
    n = inner[0].shape[0]
    slab = 16
    count = n // slab
    lane = iota((slab, n), 1)
    same = jnp.where(iota((n, n), 0) // slab == iota((n, n), 1) // slab, 1.0, 0.0)
    same_short = same.astype(BF16)

    def spread(pair):
        return tuple(rows(*[x] * count) * same_short for x in pair)

    small = [sum(jnp.where(lane // slab == i, x[i * slab : (i + 1) * slab], 0.0) for i in range(count)) for x in inner]
    solver = small_inverse(small)
    size = slab
    halves = [spread(split(x)) for x in solver]
    solver = [rows(*[x] * count) * same for x in solver]

    while size < n:
        odd = lambda x: rows(*[x[i : i + size] for i in range(size, n, 2 * size)])

        def joined(even_of, new):
            parts = []
            for i in range(0, n // 2, size):
                parts += [even_of(2 * i), new[i : i + size]]
            return rows(*parts)

        apart = odd(iota((n, n), 0) ^ iota((n, n), 1))
        joins = (apart >= size) & (apart < 2 * size)
        gap = jnp.zeros((size, n), BF16)
        mid = [square(split(jnp.where(joins, odd(x), 0.0)), t) for x, t in zip(inner, halves)]
        mid = [tuple(joined(lambda i: gap, m) for m in split(x)) for x in mid]
        later = [
            odd(x) + square((odd(t[0]), odd(t[1])), m) for x, t, m in zip(solver, halves, mid)
        ]
        halves = [
            tuple(joined(lambda i: old[i : i + size], new) for old, new in zip(t, split(x)))
            for x, t in zip(later, halves)
        ]
        solver = [joined(lambda i: x[i : i + size], y) for x, y in zip(solver, later)]
        size *= 2
    return halves


def local_kernel(*refs):
    inputs, (pieces_out, w_out, u_out) = refs[:5], refs[5:8]
    buffers = refs[8:13]
    pieces, w_all, u_all, in_sems, out_sems = refs[13:]
    n, width = w_all.shape
    order = (4, 3, 2, 0, 1)
    block = GROUP * PAIR
    groups = width // block
    loads = []
    for g in range(groups):
        here = pl.ds(g * block, block)
        loads.append(
            [
                pltpu.make_async_copy(inputs[i].at[:, here], buffers[i].at[:, here], in_sems.at[g, i])
                for i in range(5)
            ]
        )
        for i in order:
            loads[g][i].start()
    k_ref, v_ref, raw_ref, rate_ref, log_ref = buffers
    pairs = range(GROUP)
    heads = range(2 * GROUP)
    low = low_half(n)
    ones = block_ones()
    tril = tril_ones(n)
    strict = iota((n, n), 0) > iota((n, n), 1)
    row, lane = iota((CH, PAIR), 0), iota((CH, PAIR), 1)

    stores = []

    def store(slot, src, dst):
        stores.append(pltpu.make_async_copy(src, dst, out_sems.at[slot]))
        stores[-1].start()

    for g in range(groups):
        first = g * GROUP
        cut = [slice((first + p) * PAIR, (first + p + 1) * PAIR) for p in pairs]
        loads[g][4].wait()
        cumul = [decays(log_ref[:, c], tril) for c in cut]
        fall = [jnp.exp(-x) for x in cumul]
        rise = [jnp.exp(x - log_ref[:, c].astype(F32)) for x, c in zip(cumul, cut)]
        loads[g][2].wait()
        unit = [units(raw_ref[:, c], ones) for c in cut]
        alpha = [-x * y for x, y in zip(unit, rise)]
        loads[g][3].wait()
        beta = [rate_ref[:, c].astype(F32) * x * y for c, x, y in zip(cut, unit, fall)]
        loads[g][0].wait()
        key = [k_ref[:, c].astype(F32) * x for c, x in zip(cut, fall)]
        gram = [grams(alpha[p], rows(beta[p], key[p]), low) for p in pairs]
        inner, cross = [], []
        for h in heads:
            part = gram[h // 2][(h % 2) * n : (h % 2 + 1) * n]
            inner.append(jnp.where(strict, part[:, :n], 0.0))
            cross.append(jnp.where(strict, part[:, n:], 0.0))
        loads[g][1].wait()
        akv = [exact_right(split(cross[h]), v_ref[:, cut[h // 2]]) for h in heads]
        akv = [pltpu.roll(jnp.where(low, akv[2 * p], akv[2 * p + 1]), CH, 1) for p in pairs]
        right = []
        for p in pairs:
            right += [split(jnp.where(low, alpha[p], akv[p])), split(jnp.where(low, akv[p], alpha[p]))]
        solver = inverse(inner)
        solved = [square(solver[h], right[h]) for h in heads]
        w = [jnp.where(low, solved[2 * p], solved[2 * p + 1]) for p in pairs]
        u = [pltpu.roll(jnp.where(low, solved[2 * p + 1], solved[2 * p]), CH, 1) for p in pairs]
        for p in pairs:
            w_all[:, cut[p]] = w[p]
            u_all[:, cut[p]] = u[p]
            here = pl.ds((first + p) * PAIR, PAIR)
            store(4 * (first + p), w_all.at[:, here], w_out.at[:, here])
            store(4 * (first + p) + 1, u_all.at[:, here], u_out.at[:, here])
        scale = [jnp.exp(x[n - 1 :, :]) for x in cumul]
        end_b = [x * y for x, y in zip(beta, scale)]
        moved = [square(split(x.T), split(y)) for x, y in zip(end_b, w)]
        for p in pairs:
            diagonal = jnp.where(row == lane % CH, scale[p], 0.0)
            pieces[0, first + p] = jnp.where(low_half(CH), moved[p][:CH], moved[p][CH:]) + diagonal
            store(4 * (first + p) + 2, pieces.at[0, first + p], pieces_out.at[0, first + p])
        by_key = [
            mxu(v_ref[:, c].astype(F32).T.astype(BF16), lanes(*split(x * y))) for c, x, y in zip(cut, key, scale)
        ]
        fresh = [square(split(x.T), split(y)) for x, y in zip(u, end_b)]
        for p in pairs:
            end = fresh[p] + by_key[p][:, :PAIR] + by_key[p][:, PAIR:]
            pieces[1, first + p] = jnp.where(low_half(CH), end[:CH], end[CH:])
            store(4 * (first + p) + 3, pieces.at[1, first + p], pieces_out.at[1, first + p])
    for copy in stores:
        copy.wait()


def diagonal_blocks(x):
    own = (iota((PAIR, PAIR), 0) < CH) == low_half(PAIR)
    return jnp.where(own, rows(x, x), 0.0)


def square_nt(a, b):
    out = mxu(lanes(*a), rows(lanes(b[0], b[0]), lanes(b[1], b[1])), NT)
    return out[:, :PAIR] + out[:, PAIR:]


def compose_kernel(mine_ref, other_ref, late_ref, slots_ref, moves, ends, *, columns):
    late = late_ref[...] > 0.5
    low = low_half(CH)
    short = (columns + 15) // 16 * 8
    pairs = range(PAIRS)
    first = [jnp.where(late, other_ref[0, p], mine_ref[0, p]) for p in pairs]
    second = [jnp.where(late, mine_ref[0, p], other_ref[0, p]) for p in pairs]
    moved = [square(split(y), split(diagonal_blocks(x))) for x, y in zip(first, second)]
    first = [jnp.where(late, other_ref[1, p], mine_ref[1, p]) for p in pairs]
    carried = [square_nt(split(x), split(diagonal_blocks(y))) for x, y in zip(first, second)]
    for p in pairs:
        moves[p] = moved[p]
        end = carried[p] + jnp.where(late, mine_ref[1, p], other_ref[1, p])
        turned = pltpu.roll(end, CH, 1)
        ends[p * PAIR : p * PAIR + CH, :] = jnp.where(low, end, turned)
        ends[p * PAIR + CH : (p + 1) * PAIR, :] = jnp.where(low, turned, end)

    def packed(owner):
        at = owner * columns
        first, last = at // CH, (at + columns - 1) // CH
        slot = moves[first // 2]
        if first // 2 != last // 2:
            slot = jnp.where(low, moves[last // 2], slot)
        tail = rows(ends[at + short : at + columns, :], jnp.zeros((2 * short - columns, PAIR), F32))
        return slot, jnp.where(low_half(short), ends[at : at + short, :], tail)

    for chip in range(slots_ref.shape[0]):
        (move_a, end_a), (move_b, end_b) = packed(2 * chip), packed(2 * chip + 1)
        slots_ref[chip, :CH, :] = jnp.where(late, move_b, move_a)
        slots_ref[chip, CH:, :] = jnp.where(late, end_b, end_a)


def read_kernel(*refs):
    inputs, (boost_ref, shift_ref, other_ref, late_ref) = refs[:8], refs[8:12]
    outputs = refs[12:15]
    buffers = refs[15:23]
    results, in_sems, out_sems = refs[23:26], refs[26], refs[27]
    n, width = results[0].shape
    block = GROUP * PAIR
    groups = width // block

    def moved(sources, targets, sems, g):
        here = pl.ds(g * block, block)
        return [
            pltpu.make_async_copy(src.at[:, here], dst.at[:, here], sems.at[g, i])
            for i, (src, dst) in enumerate(zip(sources, targets))
        ]

    loads = [moved(inputs, buffers, in_sems, g) for g in range(groups)]
    for group in loads:
        for copy in group:
            copy.start()
    q_ref, k_ref, v_ref, raw_ref, rate_ref, log_ref, w_ref, u_ref = buffers
    read_ref, local_ref, base_ref = results
    low = low_half(n)
    ones = block_ones()
    tril = tril_ones(n)
    weak = iota((n, n), 0) >= iota((n, n), 1)
    late = late_ref[...] > 0.5
    pairs = range(GROUP)
    stores = []
    for g in range(groups):
        for copy in loads[g]:
            copy.wait()
        cut = [slice(g * block + p * PAIR, g * block + (p + 1) * PAIR) for p in pairs]
        cumul = [decays(log_ref[:, c], tril) for c in cut]
        unit = [units(raw_ref[:, c], ones) for c in cut]
        fall = [jnp.exp(-cumul[p]) for p in pairs]
        beta = [rate_ref[:, cut[p]].astype(F32) * unit[p] * fall[p] for p in pairs]
        key = [k_ref[:, cut[p]].astype(F32) * fall[p] for p in pairs]
        read = [q_ref[:, cut[p]].astype(F32) * jnp.exp(cumul[p]) for p in pairs]
        gram = [grams(read[p], rows(beta[p], key[p]), low) for p in pairs]
        for p in pairs:
            c = cut[p]
            solved = split(lanes(w_ref[:, c], u_ref[:, c]))
            v = v_ref[:, c]
            reads, locals_ = [], []
            for h in range(2):
                part = gram[p][h * n : (h + 1) * n]
                both = wide(split(jnp.where(weak, part[:, :n], 0.0)), solved)
                direct = exact_right(split(jnp.where(weak, part[:, n:], 0.0)), v)
                reads.append(both[:, :PAIR])
                locals_.append(both[:, PAIR:] + direct)
            seen = read[p] + jnp.where(low, *reads)
            here = jnp.where(low, *locals_)
            parts = split(seen)
            move, end = other_ref[0, g * GROUP + p], other_ref[1, g * GROUP + p]
            read_ref[:, c] = jnp.where(late, square(parts, split(diagonal_blocks(move))), seen)
            passed = here + square_nt(parts, split(diagonal_blocks(end)))
            local_ref[:, c] = jnp.where(late, passed, here)
            product = q_ref[:, c].astype(F32) * k_ref[:, c].astype(F32) * boost_ref[:, c]
            base_ref[:, c] = head_sum(product, ones) * v.astype(F32) + shift_ref[:, c]
        stores += moved(results, outputs, out_sems, g)
        for copy in stores[-3:]:
            copy.start()
    for copy in stores:
        copy.wait()


def scan_kernel(slots_ref, entry_ref, mask_ref, after_ref, starts_out, exit_ref, starts, sems):
    del after_ref
    count, short = slots_ref.shape[0], starts.shape[1]
    low = low_half(short)
    mask = mask_ref[...]

    def advance(state, move, fresh):
        hi, lo = split(state * mask)
        out = mxu(rows(hi, lo), rows(*move), NT)
        out = out[: 2 * short] + out[2 * short :]
        return out + pltpu.roll(out, CH, 1) + fresh

    def unpacked(d):
        end = slots_ref[d, CH:, :]
        turned = pltpu.roll(end, CH, 1)
        return rows(jnp.where(low, end, turned), jnp.where(low, turned, end))

    moves = [split(slots_ref[d, :CH, :]) for d in range(count)]
    fresh = [unpacked(d) for d in range(count)]
    both = [
        split(square(moves[d + 1], split(diagonal_blocks(slots_ref[d, :CH, :]))))
        for d in range(0, count, 2)
    ]
    joint = [advance(fresh[d], moves[d + 1], fresh[d + 1]) for d in range(0, count, 2)]
    states = [entry_ref[...]]
    for d in range(count // 2):
        states.append(advance(states[d], both[d], joint[d]))
    stores = []
    for d in range(count // 2):
        middle = advance(states[d], moves[2 * d], fresh[2 * d])
        for i, x in enumerate((states[d], middle)):
            at = 4 * d + 2 * i
            starts[at] = starts[at + 1] = jnp.where(low, x[:short], x[short:])
        part = pl.ds(4 * d, 4)
        stores.append(pltpu.make_async_copy(starts.at[part], starts_out.at[part], sems.at[d]))
        stores[-1].start()
    exit_ref[...] = states[-1]
    for copy in stores:
        copy.wait()


def final_kernel(starts_ref, read_ref, local_ref, base_ref, gain_ref, out, begins, result, out_sems, *, columns):
    cut = [slice(p * PAIR, (p + 1) * PAIR) for p in range(PAIRS)]
    place = [pl.ds(p * PAIR, PAIR) for p in range(PAIRS)]
    short = starts_ref.shape[1]
    low = low_half(short)
    for owner in range(starts_ref.shape[0]):
        part = starts_ref[owner]
        turned = pltpu.roll(part, CH, 1)
        at = owner * columns
        begins[at : at + short, :] = jnp.where(low, part, turned)
        begins[at + short : at + columns, :] = jnp.where(low, turned, part)[: columns - short]
    own = (iota((PAIR, PAIR), 0) < CH) == low_half(PAIR)
    ones = block_ones()
    right = [split(jnp.where(own, begins[c, :], 0.0)) for c in cut]
    stores = []
    for g in range(PAIRS // GROUP):
        pairs = range(g * GROUP, (g + 1) * GROUP)
        left = [split(read_ref[:, cut[p]]) for p in pairs]
        carried = [
            mxu(lanes(*a), lanes(right[p][0], right[p][0]), NT) + mxu(a[0], right[p][1], NT)
            for p, a in zip(pairs, left)
        ]
        readout = [x + local_ref[:, cut[p]] for p, x in zip(pairs, carried)]
        centred = [x - head_sum(x, ones) * (1.0 / CH) for x in readout]
        variance = [head_sum(x * x, ones) * (1.0 / CH) for x in centred]
        for p, x, y in zip(pairs, centred, variance):
            scaled = x * lax.rsqrt(y + 1e-05) * gain_ref[:, cut[p]]
            result[:, cut[p]] = (scaled + base_ref[:, cut[p]]).astype(BF16)
            stores.append(pltpu.make_async_copy(result.at[:, place[p]], out.at[:, place[p]], out_sems.at[p]))
            stores[-1].start()
    for copy in stores:
        copy.wait()


def call(kernel, **kwargs):
    params = pltpu.CompilerParams(vmem_limit_bytes=48 * 1024 * 1024)
    return pl.pallas_call(kernel, interpret=INTERPRET, compiler_params=params, **kwargs)


def shards(q, k, v, raw, rates, logs, memory, boost, gain, shift):
    n = q.shape[0]
    owners = lax.axis_size("ctx")
    columns = memory.shape[1]
    short = (columns + 15) // 16 * 8
    groups = PAIRS // GROUP
    hbm = pl.BlockSpec(memory_space=pltpu.HBM)
    held = functools.partial(pltpu.with_memory_space_constraint, memory_space=pltpu.HBM)
    vmem = pl.BlockSpec(memory_space=pltpu.VMEM)
    plane = pltpu.HBM((n, WIDTH), F32)
    arrays = [held(x) for x in (q, k, v, raw, rates, logs)]
    tokens = pltpu.VMEM((n, WIDTH), BF16)
    floats = pltpu.VMEM((n, WIDTH), F32)
    sems = pltpu.SemaphoreType.DMA

    pieces = (2, PAIRS, CH, PAIR)
    mine, w, u = call(
        local_kernel,
        in_specs=[hbm] * 5,
        out_specs=[hbm] * 3,
        out_shape=[jax.ShapeDtypeStruct(pieces, F32), plane, plane],
        scratch_shapes=[tokens] * 5
        + [pltpu.VMEM(pieces, F32), floats, floats, sems((groups, 5)), sems((4 * PAIRS,))],
    )(*arrays[1:])
    other = lax.ppermute(mine, "ctx", [(i, i ^ 1) for i in range(owners)])
    place = lax.axis_index("ctx")
    late = jnp.broadcast_to((place % 2).astype(F32), (1, PAIR))
    slots = call(
        functools.partial(compose_kernel, columns=columns),
        out_shape=jax.ShapeDtypeStruct((owners // 2, CH + short, PAIR), F32),
        scratch_shapes=[pltpu.VMEM((PAIRS, CH, PAIR), F32), pltpu.VMEM((WIDTH, PAIR), F32)],
    )(mine, other, late)
    same_core = [list(range(core, owners, 2)) for core in range(2)]
    slots = lax.all_to_all(slots, "ctx", 0, 0, axis_index_groups=same_core)

    read, local, base = call(
        read_kernel,
        in_specs=[hbm] * 8 + [vmem] * 4,
        out_specs=[hbm] * 3,
        out_shape=[jax.ShapeDtypeStruct((n, WIDTH), F32)] * 3,
        scratch_shapes=[tokens] * 6 + [floats] * 5 + [sems((groups, 8)), sems((groups, 3))],
    )(*arrays, held(w), held(u), boost.reshape(1, WIDTH), shift.reshape(1, WIDTH), other, late)

    own = lax.broadcasted_iota(jnp.int32, (2 * short, PAIR), 0)
    half = lax.broadcasted_iota(jnp.int32, (2 * short, PAIR), 1) // CH
    mask = ((place * columns + own) // CH % 2 == half) & (own < columns)
    entry = jnp.pad(memory.T, ((0, 2 * short - columns), (0, 0)))
    starts, final = call(
        scan_kernel,
        in_specs=[vmem, vmem, vmem, hbm],
        out_specs=[hbm, vmem],
        out_shape=[
            pltpu.HBM((owners, short, PAIR), F32),
            jax.ShapeDtypeStruct((2 * short, PAIR), F32),
        ],
        scratch_shapes=[pltpu.VMEM((owners, short, PAIR), F32), sems((owners // 4,))],
    )(slots, jnp.concatenate([entry, entry], axis=1), mask.astype(F32), base)
    starts = lax.all_to_all(starts, "ctx", 0, 0)
    exit_state = final[:columns, :CH].T

    out = call(
        functools.partial(final_kernel, columns=columns),
        in_specs=[vmem] * 5,
        out_specs=hbm,
        out_shape=pltpu.HBM((n, WIDTH), BF16),
        scratch_shapes=[pltpu.VMEM((WIDTH, PAIR), F32), tokens, sems((PAIRS,))],
    )(starts, read, local, base, gain.reshape(1, WIDTH))
    return out, exit_state


def solution(mesh):
    rows_spec = P(("dp", "ctx"), None)
    return jax.shard_map(
        shards,
        mesh=mesh,
        in_specs=(rows_spec,) * 6 + (P("dp", "ctx"), P(), P(), P()),
        out_specs=(rows_spec, P("dp", "ctx")),
        check_vma=False,
    )
```

```python
import functools

import jax
import jax.numpy as jnp
from jax import lax
from jax.experimental import pallas as pl
from jax.experimental.pallas import tpu as pltpu
from jax.sharding import PartitionSpec as P

HEADS = 20
CH = 64
PAIR = 2 * CH
PAIRS = HEADS // 2
WIDTH = HEADS * CH
GROUP = 5
INTERPRET = False
F32 = jnp.float32
BF16 = jnp.bfloat16
NN = (((1,), (0,)), ((), ()))
NT = (((1,), (1,)), ((), ()))


def mxu(a, b, dims=NN):
    return lax.dot_general(a, b, dims, preferred_element_type=F32)


def split(x):
    hi = x.astype(BF16)
    return hi, (x - hi.astype(F32)).astype(BF16)


def lanes(*xs):
    return jnp.concatenate(xs, axis=1)


def rows(*xs):
    return jnp.concatenate(xs, axis=0)


def square(a, b):
    both = lanes(*b)
    out = mxu(lanes(*a), rows(both, both))
    return out[:, :PAIR] + out[:, PAIR:]


def wide(a, b):
    return mxu(lanes(*a), rows(b[0], b[0])) + mxu(a[0], b[1])


def exact_right(a, b):
    return mxu(lanes(*a), rows(b, b))


def iota(shape, dim):
    return lax.broadcasted_iota(jnp.int32, shape, dim)


def low_half(n):
    return iota((n, PAIR), 1) < CH


def block_ones():
    same = (iota((PAIR, PAIR), 0) < CH) == (iota((PAIR, PAIR), 1) < CH)
    return jnp.where(same, 1.0, 0.0).astype(BF16)


def head_sum(x, ones):
    return exact_right(split(x), ones)


def decays(logs, tril):
    return mxu(tril, logs)


def units(raw, ones):
    raw = raw.astype(F32)
    return raw * lax.rsqrt(head_sum(raw * raw, ones) + CH * 1e-05)


def tril_ones(n):
    return jnp.where(iota((n, n), 0) >= iota((n, n), 1), 1.0, 0.0).astype(BF16)


def grams(left, right, low):
    first = jnp.where(low, 1.0, 0.0).astype(BF16)
    second = jnp.where(low, 0.0, 1.0).astype(BF16)
    hi, lo = (rows(x * first, x * second) for x in split(left))
    b = split(right)
    return mxu(lanes(hi, lo), lanes(b[0], b[0]), NT) + mxu(hi, b[1], NT)


def inverse(inner):
    n = inner[0].shape[0]
    slab = 16
    count = n // slab
    row, lane = iota((slab, n), 0), iota((slab, n), 1)
    apart = row ^ (lane % slab)
    same = jnp.where(iota((n, n), 0) // slab == iota((n, n), 1) // slab, 1.0, 0.0)
    same_short = same.astype(BF16)

    def spread(pair):
        return tuple(rows(*[x] * count) * same_short for x in pair)

    small = [sum(jnp.where(lane // slab == i, x[i * slab : (i + 1) * slab], 0.0) for i in range(count)) for x in inner]
    solver = [jnp.where(apart == 0, 1.0, 0.0) + jnp.where(apart == 1, x, 0.0) for x in small]
    size = 2
    while size < slab:
        joins = (apart >= size) & (apart < 2 * size)
        halves = [split(x) for x in solver]
        mid = [square(split(jnp.where(joins, x, 0.0)), spread(t)) for x, t in zip(small, halves)]
        solver = [x + square(t, spread(split(m))) for x, t, m in zip(solver, halves, mid)]
        size *= 2
    halves = [spread(split(x)) for x in solver]
    solver = [rows(*[x] * count) * same for x in solver]

    while size < n:
        odd = lambda x: rows(*[x[i : i + size] for i in range(size, n, 2 * size)])

        def joined(even_of, new):
            parts = []
            for i in range(0, n // 2, size):
                parts += [even_of(2 * i), new[i : i + size]]
            return rows(*parts)

        apart = odd(iota((n, n), 0) ^ iota((n, n), 1))
        joins = (apart >= size) & (apart < 2 * size)
        gap = jnp.zeros((size, n), BF16)
        mid = [square(split(jnp.where(joins, odd(x), 0.0)), t) for x, t in zip(inner, halves)]
        mid = [tuple(joined(lambda i: gap, m) for m in split(x)) for x in mid]
        later = [
            odd(x) + square((odd(t[0]), odd(t[1])), m) for x, t, m in zip(solver, halves, mid)
        ]
        halves = [
            tuple(joined(lambda i: old[i : i + size], new) for old, new in zip(t, split(x)))
            for x, t in zip(later, halves)
        ]
        solver = [joined(lambda i: x[i : i + size], y) for x, y in zip(solver, later)]
        size *= 2
    return halves


def local_kernel(*refs):
    inputs, (pieces, w_out, u_out) = refs[:5], refs[5:8]
    buffers = refs[8:13]
    w_all, u_all, in_sems, out_sems = refs[13:]
    n, width = w_all.shape
    block = GROUP * PAIR
    groups = width // block
    loads = [
        [
            pltpu.make_async_copy(src.at[:, pl.ds(g * block, block)], dst.at[:, pl.ds(g * block, block)], in_sems.at[g, i])
            for i, (src, dst) in enumerate(zip(inputs, buffers))
        ]
        for g in range(groups)
    ]
    for group in loads:
        for i in (4, 2, 3, 0, 1):
            group[i].start()
    k_ref, v_ref, raw_ref, rate_ref, log_ref = buffers
    low = low_half(n)
    ones = block_ones()
    tril = tril_ones(n)
    strict = iota((n, n), 0) > iota((n, n), 1)
    row, lane = iota((CH, PAIR), 0), iota((CH, PAIR), 1)
    stores = []
    pairs = range(GROUP)
    heads = range(2 * GROUP)
    for g in range(groups):
        cut = [slice(g * block + p * PAIR, g * block + (p + 1) * PAIR) for p in pairs]
        loads[g][4].wait()
        cumul = [decays(log_ref[:, c], tril) for c in cut]
        rise = [jnp.exp(cumul[p] - log_ref[:, cut[p]].astype(F32)) for p in pairs]
        fall = [jnp.exp(-cumul[p]) for p in pairs]
        loads[g][2].wait()
        unit = [units(raw_ref[:, c], ones) for c in cut]
        alpha = [-unit[p] * x for p, x in zip(pairs, rise)]
        loads[g][3].wait()
        beta = [rate_ref[:, cut[p]].astype(F32) * unit[p] * fall[p] for p in pairs]
        loads[g][0].wait()
        key = [k_ref[:, cut[p]].astype(F32) * fall[p] for p in pairs]
        gram = [grams(alpha[p], rows(beta[p], key[p]), low) for p in pairs]

        inner, cross = [], []
        for h in heads:
            part = gram[h // 2][(h % 2) * n : (h % 2 + 1) * n]
            inner.append(jnp.where(strict, part[:, :n], 0.0))
            cross.append(jnp.where(strict, part[:, n:], 0.0))
        loads[g][1].wait()
        akv = [exact_right(split(cross[h]), v_ref[:, cut[h // 2]]) for h in heads]
        akv = [jnp.where(low, akv[2 * p], akv[2 * p + 1]) for p in pairs]
        right = [split(lanes(alpha[p], akv[p])) for p in pairs]
        solver = inverse(inner)
        solved = [wide(solver[h], right[h // 2]) for h in heads]
        for p in pairs:
            first, second = solved[2 * p], solved[2 * p + 1]
            w = jnp.where(low, first[:, :PAIR], second[:, :PAIR])
            u = jnp.where(low, first[:, PAIR:], second[:, PAIR:])
            w_all[:, cut[p]] = w
            u_all[:, cut[p]] = u
        here = pl.ds(g * block, block)
        stores += [
            pltpu.make_async_copy(w_all.at[:, here], w_out.at[:, here], out_sems.at[g, 0]),
            pltpu.make_async_copy(u_all.at[:, here], u_out.at[:, here], out_sems.at[g, 1]),
        ]
        for copy in stores[-2:]:
            copy.start()
        for p in pairs:
            w, u = w_all[:, cut[p]], u_all[:, cut[p]]
            scale = jnp.exp(cumul[p][n - 1 :, :])
            end_b = beta[p] * scale
            end_k = key[p] * scale
            moved = square(split(end_b.T), split(w))
            diagonal = jnp.where(row == lane % CH, scale, 0.0)
            pieces[0, g * GROUP + p] = jnp.where(low_half(CH), moved[:CH], moved[CH:]) + diagonal
            content = v_ref[:, cut[p]].astype(F32).T.astype(BF16)
            by_key = mxu(content, lanes(*split(end_k)))
            fresh = square(split(u.T), split(end_b)) + by_key[:, :PAIR] + by_key[:, PAIR:]
            pieces[1, g * GROUP + p] = jnp.where(low_half(CH), fresh[:CH], fresh[CH:])
    for copy in stores:
        copy.wait()


def diagonal_blocks(x):
    own = (iota((PAIR, PAIR), 0) < CH) == low_half(PAIR)
    return jnp.where(own, rows(x, x), 0.0)


def square_nt(a, b):
    out = mxu(lanes(*a), rows(lanes(b[0], b[0]), lanes(b[1], b[1])), NT)
    return out[:, :PAIR] + out[:, PAIR:]


def compose_kernel(mine_ref, other_ref, late_ref, slots_ref, moves, ends, *, columns):
    late = late_ref[...] > 0.5
    low = low_half(CH)
    short = (columns + 15) // 16 * 8
    pairs = range(PAIRS)
    first = [jnp.where(late, other_ref[0, p], mine_ref[0, p]) for p in pairs]
    second = [jnp.where(late, mine_ref[0, p], other_ref[0, p]) for p in pairs]
    moved = [square(split(y), split(diagonal_blocks(x))) for x, y in zip(first, second)]
    first = [jnp.where(late, other_ref[1, p], mine_ref[1, p]) for p in pairs]
    carried = [square_nt(split(x), split(diagonal_blocks(y))) for x, y in zip(first, second)]
    for p in pairs:
        moves[p] = moved[p]
        end = carried[p] + jnp.where(late, mine_ref[1, p], other_ref[1, p])
        turned = pltpu.roll(end, CH, 1)
        ends[p * PAIR : p * PAIR + CH, :] = jnp.where(low, end, turned)
        ends[p * PAIR + CH : (p + 1) * PAIR, :] = jnp.where(low, turned, end)

    def packed(owner):
        at = owner * columns
        first, last = at // CH, (at + columns - 1) // CH
        slot = moves[first // 2]
        if first // 2 != last // 2:
            slot = jnp.where(low, moves[last // 2], slot)
        tail = rows(ends[at + short : at + columns, :], jnp.zeros((2 * short - columns, PAIR), F32))
        return slot, jnp.where(low_half(short), ends[at : at + short, :], tail)

    for chip in range(slots_ref.shape[0]):
        (move_a, end_a), (move_b, end_b) = packed(2 * chip), packed(2 * chip + 1)
        slots_ref[chip, :CH, :] = jnp.where(late, move_b, move_a)
        slots_ref[chip, CH:, :] = jnp.where(late, end_b, end_a)


def read_kernel(*refs):
    inputs, (boost_ref, shift_ref, other_ref, late_ref) = refs[:8], refs[8:12]
    outputs = refs[12:15]
    buffers = refs[15:23]
    results, in_sems, out_sems = refs[23:26], refs[26], refs[27]
    n, width = results[0].shape
    block = GROUP * PAIR
    groups = width // block

    def moved(sources, targets, sems, g):
        here = pl.ds(g * block, block)
        return [
            pltpu.make_async_copy(src.at[:, here], dst.at[:, here], sems.at[g, i])
            for i, (src, dst) in enumerate(zip(sources, targets))
        ]

    loads = [moved(inputs, buffers, in_sems, g) for g in range(groups)]
    for group in loads:
        for copy in group:
            copy.start()
    q_ref, k_ref, v_ref, raw_ref, rate_ref, log_ref, w_ref, u_ref = buffers
    read_ref, local_ref, base_ref = results
    low = low_half(n)
    ones = block_ones()
    tril = tril_ones(n)
    weak = iota((n, n), 0) >= iota((n, n), 1)
    late = late_ref[...] > 0.5
    pairs = range(GROUP)
    stores = []
    for g in range(groups):
        for copy in loads[g]:
            copy.wait()
        cut = [slice(g * block + p * PAIR, g * block + (p + 1) * PAIR) for p in pairs]
        cumul = [decays(log_ref[:, c], tril) for c in cut]
        unit = [units(raw_ref[:, c], ones) for c in cut]
        fall = [jnp.exp(-cumul[p]) for p in pairs]
        beta = [rate_ref[:, cut[p]].astype(F32) * unit[p] * fall[p] for p in pairs]
        key = [k_ref[:, cut[p]].astype(F32) * fall[p] for p in pairs]
        read = [q_ref[:, cut[p]].astype(F32) * jnp.exp(cumul[p]) for p in pairs]
        gram = [grams(read[p], rows(beta[p], key[p]), low) for p in pairs]
        for p in pairs:
            c = cut[p]
            solved = split(lanes(w_ref[:, c], u_ref[:, c]))
            v = v_ref[:, c]
            reads, locals_ = [], []
            for h in range(2):
                part = gram[p][h * n : (h + 1) * n]
                both = wide(split(jnp.where(weak, part[:, :n], 0.0)), solved)
                direct = exact_right(split(jnp.where(weak, part[:, n:], 0.0)), v)
                reads.append(both[:, :PAIR])
                locals_.append(both[:, PAIR:] + direct)
            seen = read[p] + jnp.where(low, *reads)
            here = jnp.where(low, *locals_)
            parts = split(seen)
            move, end = other_ref[0, g * GROUP + p], other_ref[1, g * GROUP + p]
            read_ref[:, c] = jnp.where(late, square(parts, split(diagonal_blocks(move))), seen)
            passed = here + square_nt(parts, split(diagonal_blocks(end)))
            local_ref[:, c] = jnp.where(late, passed, here)
            product = q_ref[:, c].astype(F32) * k_ref[:, c].astype(F32) * boost_ref[:, c]
            base_ref[:, c] = head_sum(product, ones) * v.astype(F32) + shift_ref[:, c]
        stores += moved(results, outputs, out_sems, g)
        for copy in stores[-3:]:
            copy.start()
    for copy in stores:
        copy.wait()


def scan_kernel(slots_ref, entry_ref, mask_ref, after_ref, starts_out, exit_ref, starts, sems):
    del after_ref
    count, short = slots_ref.shape[0], starts.shape[1]
    low = low_half(short)
    mask = mask_ref[...]

    def weights(move):
        hi, lo = move
        return rows(lanes(hi, hi), lanes(hi, hi), lanes(lo, lo), lanes(lo, lo))

    def advance(state, move, fresh):
        out = mxu(lanes(*split(state * mask)), move, NT)
        return out[:, :PAIR] + out[:, PAIR:] + fresh

    def unpacked(d):
        end = slots_ref[d, CH:, :]
        turned = pltpu.roll(end, CH, 1)
        return rows(jnp.where(low, end, turned), jnp.where(low, turned, end))

    parts = [split(slots_ref[d, :CH, :]) for d in range(count)]
    moves = [weights(x) for x in parts]
    fresh = [unpacked(d) for d in range(count)]
    both = [
        weights(split(square(parts[d + 1], split(diagonal_blocks(slots_ref[d, :CH, :])))))
        for d in range(0, count, 2)
    ]
    joint = [advance(fresh[d], moves[d + 1], fresh[d + 1]) for d in range(0, count, 2)]
    state = entry_ref[...]
    stores = []
    for d in range(count // 2):
        following = advance(state, both[d], joint[d])
        middle = advance(state, moves[2 * d], fresh[2 * d])
        for i, x in enumerate((state, middle)):
            at = 4 * d + 2 * i
            starts[at] = starts[at + 1] = jnp.where(low, x[:short], x[short:])
        part = pl.ds(4 * d, 4)
        stores.append(pltpu.make_async_copy(starts.at[part], starts_out.at[part], sems.at[d]))
        stores[-1].start()
        state = following
    exit_ref[...] = state
    for copy in stores:
        copy.wait()


def final_kernel(starts_ref, read_ref, local_ref, base_ref, gain_ref, out, begins, result, out_sems, *, columns):
    cut = [slice(p * PAIR, (p + 1) * PAIR) for p in range(PAIRS)]
    place = [pl.ds(p * PAIR, PAIR) for p in range(PAIRS)]
    short = starts_ref.shape[1]
    low = low_half(short)
    for owner in range(starts_ref.shape[0]):
        part = starts_ref[owner]
        turned = pltpu.roll(part, CH, 1)
        at = owner * columns
        begins[at : at + short, :] = jnp.where(low, part, turned)
        begins[at + short : at + columns, :] = jnp.where(low, turned, part)[: columns - short]
    own = (iota((PAIR, PAIR), 0) < CH) == low_half(PAIR)
    ones = block_ones()
    right = [split(jnp.where(own, begins[c, :], 0.0)) for c in cut]
    stores = []
    for g in range(PAIRS // GROUP):
        pairs = range(g * GROUP, (g + 1) * GROUP)
        left = [split(read_ref[:, cut[p]]) for p in pairs]
        carried = [
            mxu(lanes(*a), lanes(right[p][0], right[p][0]), NT) + mxu(a[0], right[p][1], NT)
            for p, a in zip(pairs, left)
        ]
        readout = [x + local_ref[:, cut[p]] for p, x in zip(pairs, carried)]
        centred = [x - head_sum(x, ones) * (1.0 / CH) for x in readout]
        variance = [head_sum(x * x, ones) * (1.0 / CH) for x in centred]
        for p, x, y in zip(pairs, centred, variance):
            scaled = x * lax.rsqrt(y + 1e-05) * gain_ref[:, cut[p]]
            result[:, cut[p]] = (scaled + base_ref[:, cut[p]]).astype(BF16)
            stores.append(pltpu.make_async_copy(result.at[:, place[p]], out.at[:, place[p]], out_sems.at[p]))
            stores[-1].start()
    for copy in stores:
        copy.wait()


def call(kernel, **kwargs):
    params = pltpu.CompilerParams(vmem_limit_bytes=48 * 1024 * 1024)
    return pl.pallas_call(kernel, interpret=INTERPRET, compiler_params=params, **kwargs)


def shards(q, k, v, raw, rates, logs, memory, boost, gain, shift):
    n = q.shape[0]
    owners = lax.axis_size("ctx")
    columns = memory.shape[1]
    short = (columns + 15) // 16 * 8
    groups = PAIRS // GROUP
    hbm = pl.BlockSpec(memory_space=pltpu.HBM)
    held = functools.partial(pltpu.with_memory_space_constraint, memory_space=pltpu.HBM)
    vmem = pl.BlockSpec(memory_space=pltpu.VMEM)
    plane = pltpu.HBM((n, WIDTH), F32)
    arrays = [held(x) for x in (q, k, v, raw, rates, logs)]
    tokens = pltpu.VMEM((n, WIDTH), BF16)
    floats = pltpu.VMEM((n, WIDTH), F32)
    sems = pltpu.SemaphoreType.DMA

    pieces = (2, PAIRS, CH, PAIR)
    mine, w, u = call(
        local_kernel,
        in_specs=[hbm] * 5,
        out_specs=[vmem, hbm, hbm],
        out_shape=[jax.ShapeDtypeStruct(pieces, F32), plane, plane],
        scratch_shapes=[tokens] * 5
        + [floats, floats, sems((groups, 5)), sems((groups, 2))],
    )(*arrays[1:])
    other = lax.ppermute(mine, "ctx", [(i, i ^ 1) for i in range(owners)])
    place = lax.axis_index("ctx")
    late = jnp.broadcast_to((place % 2).astype(F32), (1, PAIR))
    slots = call(
        functools.partial(compose_kernel, columns=columns),
        out_shape=jax.ShapeDtypeStruct((owners // 2, CH + short, PAIR), F32),
        scratch_shapes=[pltpu.VMEM((PAIRS, CH, PAIR), F32), pltpu.VMEM((WIDTH, PAIR), F32)],
    )(mine, other, late)
    same_core = [list(range(core, owners, 2)) for core in range(2)]
    slots = lax.all_to_all(slots, "ctx", 0, 0, axis_index_groups=same_core)

    read, local, base = call(
        read_kernel,
        in_specs=[hbm] * 8 + [vmem] * 4,
        out_specs=[hbm] * 3,
        out_shape=[jax.ShapeDtypeStruct((n, WIDTH), F32)] * 3,
        scratch_shapes=[tokens] * 6 + [floats] * 5 + [sems((groups, 8)), sems((groups, 3))],
    )(*arrays, held(w), held(u), boost.reshape(1, WIDTH), shift.reshape(1, WIDTH), other, late)

    own = lax.broadcasted_iota(jnp.int32, (2 * short, PAIR), 0)
    half = lax.broadcasted_iota(jnp.int32, (2 * short, PAIR), 1) // CH
    mask = ((place * columns + own) // CH % 2 == half) & (own < columns)
    entry = jnp.pad(memory.T, ((0, 2 * short - columns), (0, 0)))
    starts, final = call(
        scan_kernel,
        in_specs=[vmem, vmem, vmem, hbm],
        out_specs=[hbm, vmem],
        out_shape=[
            pltpu.HBM((owners, short, PAIR), F32),
            jax.ShapeDtypeStruct((2 * short, PAIR), F32),
        ],
        scratch_shapes=[pltpu.VMEM((owners, short, PAIR), F32), sems((owners // 4,))],
    )(slots, jnp.concatenate([entry, entry], axis=1), mask.astype(F32), base)
    starts = lax.all_to_all(starts, "ctx", 0, 0)
    exit_state = final[:columns, :CH].T

    out = call(
        functools.partial(final_kernel, columns=columns),
        in_specs=[vmem] * 5,
        out_specs=hbm,
        out_shape=pltpu.HBM((n, WIDTH), BF16),
        scratch_shapes=[pltpu.VMEM((WIDTH, PAIR), F32), tokens, sems((PAIRS,))],
    )(starts, read, local, base, gain.reshape(1, WIDTH))
    return out, exit_state


def solution(mesh):
    rows_spec = P(("dp", "ctx"), None)
    return jax.shard_map(
        shards,
        mesh=mesh,
        in_specs=(rows_spec,) * 6 + (P("dp", "ctx"), P(), P(), P()),
        out_specs=(rows_spec, P("dp", "ctx")),
        check_vma=False,
    )
```

```python
import functools

import jax
import jax.numpy as jnp
from jax import lax
from jax.experimental import pallas as pl
from jax.experimental.pallas import tpu as pltpu
from jax.sharding import PartitionSpec as P

HEADS = 20
CH = 64
PAIR = 2 * CH
PAIRS = HEADS // 2
WIDTH = HEADS * CH
GROUP = 5
INTERPRET = False
F32 = jnp.float32
BF16 = jnp.bfloat16
NN = (((1,), (0,)), ((), ()))
NT = (((1,), (1,)), ((), ()))


def mxu(a, b, dims=NN):
    return lax.dot_general(a, b, dims, preferred_element_type=F32)


def split(x):
    hi = x.astype(BF16)
    return hi, (x - hi.astype(F32)).astype(BF16)


def lanes(*xs):
    return jnp.concatenate(xs, axis=1)


def rows(*xs):
    return jnp.concatenate(xs, axis=0)


def square(a, b):
    both = lanes(*b)
    out = mxu(lanes(*a), rows(both, both))
    return out[:, :PAIR] + out[:, PAIR:]


def wide(a, b):
    return mxu(lanes(*a), rows(b[0], b[0])) + mxu(a[0], b[1])


def exact_right(a, b):
    return mxu(lanes(*a), rows(b, b))


def iota(shape, dim):
    return lax.broadcasted_iota(jnp.int32, shape, dim)


def low_half(n):
    return iota((n, PAIR), 1) < CH


def block_ones():
    same = (iota((PAIR, PAIR), 0) < CH) == (iota((PAIR, PAIR), 1) < CH)
    return jnp.where(same, 1.0, 0.0).astype(BF16)


def head_sum(x, ones):
    return exact_right(split(x), ones)


def decays(logs, tril):
    return mxu(tril, logs)


def units(raw, ones):
    raw = raw.astype(F32)
    return raw * lax.rsqrt(head_sum(raw * raw, ones) + CH * 1e-05)


def tril_ones(n):
    return jnp.where(iota((n, n), 0) >= iota((n, n), 1), 1.0, 0.0).astype(BF16)


def grams(left, right, low):
    first = jnp.where(low, 1.0, 0.0).astype(BF16)
    second = jnp.where(low, 0.0, 1.0).astype(BF16)
    hi, lo = (rows(x * first, x * second) for x in split(left))
    b = split(right)
    return mxu(lanes(hi, lo), lanes(b[0], b[0]), NT) + mxu(hi, b[1], NT)


def inverse(inner):
    n = inner[0].shape[0]
    slab = 16
    count = n // slab
    row, lane = iota((slab, n), 0), iota((slab, n), 1)
    apart = row ^ (lane % slab)
    same = jnp.where(iota((n, n), 0) // slab == iota((n, n), 1) // slab, 1.0, 0.0)
    same_short = same.astype(BF16)

    def spread(pair):
        return tuple(rows(*[x] * count) * same_short for x in pair)

    small = [sum(jnp.where(lane // slab == i, x[i * slab : (i + 1) * slab], 0.0) for i in range(count)) for x in inner]
    solver = [jnp.where(apart == 0, 1.0, 0.0) + jnp.where(apart == 1, x, 0.0) for x in small]
    size = 2
    while size < slab:
        joins = (apart >= size) & (apart < 2 * size)
        halves = [split(x) for x in solver]
        mid = [square(split(jnp.where(joins, x, 0.0)), spread(t)) for x, t in zip(small, halves)]
        solver = [x + square(t, spread(split(m))) for x, t, m in zip(solver, halves, mid)]
        size *= 2
    halves = [spread(split(x)) for x in solver]
    solver = [rows(*[x] * count) * same for x in solver]

    while size < n:
        odd = lambda x: rows(*[x[i : i + size] for i in range(size, n, 2 * size)])

        def joined(even_of, new):
            parts = []
            for i in range(0, n // 2, size):
                parts += [even_of(2 * i), new[i : i + size]]
            return rows(*parts)

        apart = odd(iota((n, n), 0) ^ iota((n, n), 1))
        joins = (apart >= size) & (apart < 2 * size)
        gap = jnp.zeros((size, n), BF16)
        mid = [square(split(jnp.where(joins, odd(x), 0.0)), t) for x, t in zip(inner, halves)]
        mid = [tuple(joined(lambda i: gap, m) for m in split(x)) for x in mid]
        later = [
            odd(x) + square((odd(t[0]), odd(t[1])), m) for x, t, m in zip(solver, halves, mid)
        ]
        halves = [
            tuple(joined(lambda i: old[i : i + size], new) for old, new in zip(t, split(x)))
            for x, t in zip(later, halves)
        ]
        solver = [joined(lambda i: x[i : i + size], y) for x, y in zip(solver, later)]
        size *= 2
    return halves


def local_kernel(*refs):
    inputs, (pieces, w_out, u_out) = refs[:5], refs[5:8]
    buffers = refs[8:13]
    w_all, u_all, in_sems, out_sems = refs[13:]
    n, width = w_all.shape
    block = GROUP * PAIR
    groups = width // block
    loads = [
        [
            pltpu.make_async_copy(src.at[:, pl.ds(g * block, block)], dst.at[:, pl.ds(g * block, block)], in_sems.at[g, i])
            for i, (src, dst) in enumerate(zip(inputs, buffers))
        ]
        for g in range(groups)
    ]
    for group in loads:
        for i in (4, 2, 3, 0, 1):
            group[i].start()
    for group in loads:
        for copy in group:
            copy.wait()
    k_ref, v_ref, raw_ref, rate_ref, log_ref = buffers
    low = low_half(n)
    ones = block_ones()
    tril = tril_ones(n)
    strict = iota((n, n), 0) > iota((n, n), 1)
    row, lane = iota((CH, PAIR), 0), iota((CH, PAIR), 1)
    stores = []
    pairs = range(GROUP)
    heads = range(2 * GROUP)
    for g in range(groups):
        cut = [slice(g * block + p * PAIR, g * block + (p + 1) * PAIR) for p in pairs]
        cumul = [decays(log_ref[:, c], tril) for c in cut]
        rise = [jnp.exp(cumul[p] - log_ref[:, cut[p]].astype(F32)) for p in pairs]
        fall = [jnp.exp(-cumul[p]) for p in pairs]
        unit = [units(raw_ref[:, c], ones) for c in cut]
        alpha = [-unit[p] * x for p, x in zip(pairs, rise)]
        beta = [rate_ref[:, cut[p]].astype(F32) * unit[p] * fall[p] for p in pairs]
        key = [k_ref[:, cut[p]].astype(F32) * fall[p] for p in pairs]
        gram = [grams(alpha[p], rows(beta[p], key[p]), low) for p in pairs]

        inner, cross = [], []
        for h in heads:
            part = gram[h // 2][(h % 2) * n : (h % 2 + 1) * n]
            inner.append(jnp.where(strict, part[:, :n], 0.0))
            cross.append(jnp.where(strict, part[:, n:], 0.0))
        akv = [exact_right(split(cross[h]), v_ref[:, cut[h // 2]]) for h in heads]
        akv = [jnp.where(low, akv[2 * p], akv[2 * p + 1]) for p in pairs]
        right = [split(lanes(alpha[p], akv[p])) for p in pairs]
        solver = inverse(inner)
        solved = [wide(solver[h], right[h // 2]) for h in heads]
        for p in pairs:
            first, second = solved[2 * p], solved[2 * p + 1]
            w = jnp.where(low, first[:, :PAIR], second[:, :PAIR])
            u = jnp.where(low, first[:, PAIR:], second[:, PAIR:])
            w_all[:, cut[p]] = w
            u_all[:, cut[p]] = u
        here = pl.ds(g * block, block)
        stores += [
            pltpu.make_async_copy(w_all.at[:, here], w_out.at[:, here], out_sems.at[g, 0]),
            pltpu.make_async_copy(u_all.at[:, here], u_out.at[:, here], out_sems.at[g, 1]),
        ]
        for copy in stores[-2:]:
            copy.start()
        for p in pairs:
            w, u = w_all[:, cut[p]], u_all[:, cut[p]]
            scale = jnp.exp(cumul[p][n - 1 :, :])
            end_b = beta[p] * scale
            end_k = key[p] * scale
            moved = square(split(end_b.T), split(w))
            diagonal = jnp.where(row == lane % CH, scale, 0.0)
            pieces[0, g * GROUP + p] = jnp.where(low_half(CH), moved[:CH], moved[CH:]) + diagonal
            content = v_ref[:, cut[p]].astype(F32).T.astype(BF16)
            by_key = mxu(content, lanes(*split(end_k)))
            fresh = square(split(u.T), split(end_b)) + by_key[:, :PAIR] + by_key[:, PAIR:]
            pieces[1, g * GROUP + p] = jnp.where(low_half(CH), fresh[:CH], fresh[CH:])
    for copy in stores:
        copy.wait()


def diagonal_blocks(x):
    own = (iota((PAIR, PAIR), 0) < CH) == low_half(PAIR)
    return jnp.where(own, rows(x, x), 0.0)


def square_nt(a, b):
    out = mxu(lanes(*a), rows(lanes(b[0], b[0]), lanes(b[1], b[1])), NT)
    return out[:, :PAIR] + out[:, PAIR:]


def compose_kernel(mine_ref, other_ref, late_ref, slots_ref, moves, ends, *, columns):
    late = late_ref[...] > 0.5
    low = low_half(CH)
    short = (columns + 15) // 16 * 8
    pairs = range(PAIRS)
    first = [jnp.where(late, other_ref[0, p], mine_ref[0, p]) for p in pairs]
    second = [jnp.where(late, mine_ref[0, p], other_ref[0, p]) for p in pairs]
    moved = [square(split(y), split(diagonal_blocks(x))) for x, y in zip(first, second)]
    first = [jnp.where(late, other_ref[1, p], mine_ref[1, p]) for p in pairs]
    carried = [square_nt(split(x), split(diagonal_blocks(y))) for x, y in zip(first, second)]
    for p in pairs:
        moves[p] = moved[p]
        end = carried[p] + jnp.where(late, mine_ref[1, p], other_ref[1, p])
        turned = pltpu.roll(end, CH, 1)
        ends[p * PAIR : p * PAIR + CH, :] = jnp.where(low, end, turned)
        ends[p * PAIR + CH : (p + 1) * PAIR, :] = jnp.where(low, turned, end)

    def packed(owner):
        at = owner * columns
        first, last = at // CH, (at + columns - 1) // CH
        slot = moves[first // 2]
        if first // 2 != last // 2:
            slot = jnp.where(low, moves[last // 2], slot)
        tail = rows(ends[at + short : at + columns, :], jnp.zeros((2 * short - columns, PAIR), F32))
        return slot, jnp.where(low_half(short), ends[at : at + short, :], tail)

    for chip in range(slots_ref.shape[0]):
        (move_a, end_a), (move_b, end_b) = packed(2 * chip), packed(2 * chip + 1)
        slots_ref[chip, :CH, :] = jnp.where(late, move_b, move_a)
        slots_ref[chip, CH:, :] = jnp.where(late, end_b, end_a)


def read_kernel(*refs):
    inputs, (boost_ref, shift_ref, other_ref, late_ref) = refs[:8], refs[8:12]
    outputs = refs[12:15]
    buffers = refs[15:23]
    results, in_sems, out_sems = refs[23:26], refs[26], refs[27]
    n, width = results[0].shape
    block = GROUP * PAIR
    groups = width // block

    def moved(sources, targets, sems, g):
        here = pl.ds(g * block, block)
        return [
            pltpu.make_async_copy(src.at[:, here], dst.at[:, here], sems.at[g, i])
            for i, (src, dst) in enumerate(zip(sources, targets))
        ]

    loads = [moved(inputs, buffers, in_sems, g) for g in range(groups)]
    for group in loads:
        for copy in group:
            copy.start()
    q_ref, k_ref, v_ref, raw_ref, rate_ref, log_ref, w_ref, u_ref = buffers
    read_ref, local_ref, base_ref = results
    low = low_half(n)
    ones = block_ones()
    tril = tril_ones(n)
    weak = iota((n, n), 0) >= iota((n, n), 1)
    late = late_ref[...] > 0.5
    pairs = range(GROUP)
    stores = []
    for g in range(groups):
        for copy in loads[g]:
            copy.wait()
        cut = [slice(g * block + p * PAIR, g * block + (p + 1) * PAIR) for p in pairs]
        cumul = [decays(log_ref[:, c], tril) for c in cut]
        unit = [units(raw_ref[:, c], ones) for c in cut]
        fall = [jnp.exp(-cumul[p]) for p in pairs]
        beta = [rate_ref[:, cut[p]].astype(F32) * unit[p] * fall[p] for p in pairs]
        key = [k_ref[:, cut[p]].astype(F32) * fall[p] for p in pairs]
        read = [q_ref[:, cut[p]].astype(F32) * jnp.exp(cumul[p]) for p in pairs]
        gram = [grams(read[p], rows(beta[p], key[p]), low) for p in pairs]
        for p in pairs:
            c = cut[p]
            solved = split(lanes(w_ref[:, c], u_ref[:, c]))
            v = v_ref[:, c]
            reads, locals_ = [], []
            for h in range(2):
                part = gram[p][h * n : (h + 1) * n]
                both = wide(split(jnp.where(weak, part[:, :n], 0.0)), solved)
                direct = exact_right(split(jnp.where(weak, part[:, n:], 0.0)), v)
                reads.append(both[:, :PAIR])
                locals_.append(both[:, PAIR:] + direct)
            seen = read[p] + jnp.where(low, *reads)
            here = jnp.where(low, *locals_)
            parts = split(seen)
            move, end = other_ref[0, g * GROUP + p], other_ref[1, g * GROUP + p]
            read_ref[:, c] = jnp.where(late, square(parts, split(diagonal_blocks(move))), seen)
            passed = here + square_nt(parts, split(diagonal_blocks(end)))
            local_ref[:, c] = jnp.where(late, passed, here)
            product = q_ref[:, c].astype(F32) * k_ref[:, c].astype(F32) * boost_ref[:, c]
            base_ref[:, c] = head_sum(product, ones) * v.astype(F32) + shift_ref[:, c]
        stores += moved(results, outputs, out_sems, g)
        for copy in stores[-3:]:
            copy.start()
    for copy in stores:
        copy.wait()


def scan_kernel(slots_ref, entry_ref, mask_ref, after_ref, starts_out, exit_ref, starts, sems):
    del after_ref
    count, short = slots_ref.shape[0], starts.shape[1]
    low = low_half(short)
    mask = mask_ref[...]

    def weights(move):
        hi, lo = move
        return rows(lanes(hi, hi), lanes(hi, hi), lanes(lo, lo), lanes(lo, lo))

    def advance(state, move, fresh):
        out = mxu(lanes(*split(state * mask)), move, NT)
        return out[:, :PAIR] + out[:, PAIR:] + fresh

    def unpacked(d):
        end = slots_ref[d, CH:, :]
        turned = pltpu.roll(end, CH, 1)
        return rows(jnp.where(low, end, turned), jnp.where(low, turned, end))

    parts = [split(slots_ref[d, :CH, :]) for d in range(count)]
    moves = [weights(x) for x in parts]
    fresh = [unpacked(d) for d in range(count)]
    both = [
        weights(split(square(parts[d + 1], split(diagonal_blocks(slots_ref[d, :CH, :])))))
        for d in range(0, count, 2)
    ]
    joint = [advance(fresh[d], moves[d + 1], fresh[d + 1]) for d in range(0, count, 2)]
    state = entry_ref[...]
    stores = []
    for d in range(count // 2):
        following = advance(state, both[d], joint[d])
        middle = advance(state, moves[2 * d], fresh[2 * d])
        for i, x in enumerate((state, middle)):
            at = 4 * d + 2 * i
            starts[at] = starts[at + 1] = jnp.where(low, x[:short], x[short:])
        part = pl.ds(4 * d, 4)
        stores.append(pltpu.make_async_copy(starts.at[part], starts_out.at[part], sems.at[d]))
        stores[-1].start()
        state = following
    exit_ref[...] = state
    for copy in stores:
        copy.wait()


def final_kernel(starts_ref, read_ref, local_ref, base_ref, gain_ref, out, begins, result, out_sems, *, columns):
    cut = [slice(p * PAIR, (p + 1) * PAIR) for p in range(PAIRS)]
    place = [pl.ds(p * PAIR, PAIR) for p in range(PAIRS)]
    short = starts_ref.shape[1]
    low = low_half(short)
    for owner in range(starts_ref.shape[0]):
        part = starts_ref[owner]
        turned = pltpu.roll(part, CH, 1)
        at = owner * columns
        begins[at : at + short, :] = jnp.where(low, part, turned)
        begins[at + short : at + columns, :] = jnp.where(low, turned, part)[: columns - short]
    own = (iota((PAIR, PAIR), 0) < CH) == low_half(PAIR)
    ones = block_ones()
    right = [split(jnp.where(own, begins[c, :], 0.0)) for c in cut]
    stores = []
    for g in range(PAIRS // GROUP):
        pairs = range(g * GROUP, (g + 1) * GROUP)
        left = [split(read_ref[:, cut[p]]) for p in pairs]
        carried = [
            mxu(lanes(*a), lanes(right[p][0], right[p][0]), NT) + mxu(a[0], right[p][1], NT)
            for p, a in zip(pairs, left)
        ]
        readout = [x + local_ref[:, cut[p]] for p, x in zip(pairs, carried)]
        centred = [x - head_sum(x, ones) * (1.0 / CH) for x in readout]
        variance = [head_sum(x * x, ones) * (1.0 / CH) for x in centred]
        for p, x, y in zip(pairs, centred, variance):
            scaled = x * lax.rsqrt(y + 1e-05) * gain_ref[:, cut[p]]
            result[:, cut[p]] = (scaled + base_ref[:, cut[p]]).astype(BF16)
            stores.append(pltpu.make_async_copy(result.at[:, place[p]], out.at[:, place[p]], out_sems.at[p]))
            stores[-1].start()
    for copy in stores:
        copy.wait()


def call(kernel, **kwargs):
    params = pltpu.CompilerParams(vmem_limit_bytes=48 * 1024 * 1024)
    return pl.pallas_call(kernel, interpret=INTERPRET, compiler_params=params, **kwargs)


def shards(q, k, v, raw, rates, logs, memory, boost, gain, shift):
    n = q.shape[0]
    owners = lax.axis_size("ctx")
    columns = memory.shape[1]
    short = (columns + 15) // 16 * 8
    groups = PAIRS // GROUP
    hbm = pl.BlockSpec(memory_space=pltpu.HBM)
    held = functools.partial(pltpu.with_memory_space_constraint, memory_space=pltpu.HBM)
    vmem = pl.BlockSpec(memory_space=pltpu.VMEM)
    plane = pltpu.HBM((n, WIDTH), F32)
    arrays = [held(x) for x in (q, k, v, raw, rates, logs)]
    tokens = pltpu.VMEM((n, WIDTH), BF16)
    floats = pltpu.VMEM((n, WIDTH), F32)
    sems = pltpu.SemaphoreType.DMA

    pieces = (2, PAIRS, CH, PAIR)
    mine, w, u = call(
        local_kernel,
        in_specs=[hbm] * 5,
        out_specs=[vmem, hbm, hbm],
        out_shape=[jax.ShapeDtypeStruct(pieces, F32), plane, plane],
        scratch_shapes=[tokens] * 5
        + [floats, floats, sems((groups, 5)), sems((groups, 2))],
    )(*arrays[1:])
    other = lax.ppermute(mine, "ctx", [(i, i ^ 1) for i in range(owners)])
    place = lax.axis_index("ctx")
    late = jnp.broadcast_to((place % 2).astype(F32), (1, PAIR))
    slots = call(
        functools.partial(compose_kernel, columns=columns),
        out_shape=jax.ShapeDtypeStruct((owners // 2, CH + short, PAIR), F32),
        scratch_shapes=[pltpu.VMEM((PAIRS, CH, PAIR), F32), pltpu.VMEM((WIDTH, PAIR), F32)],
    )(mine, other, late)
    same_core = [list(range(core, owners, 2)) for core in range(2)]
    slots = lax.all_to_all(slots, "ctx", 0, 0, axis_index_groups=same_core)

    read, local, base = call(
        read_kernel,
        in_specs=[hbm] * 8 + [vmem] * 4,
        out_specs=[hbm] * 3,
        out_shape=[jax.ShapeDtypeStruct((n, WIDTH), F32)] * 3,
        scratch_shapes=[tokens] * 6 + [floats] * 5 + [sems((groups, 8)), sems((groups, 3))],
    )(*arrays, held(w), held(u), boost.reshape(1, WIDTH), shift.reshape(1, WIDTH), other, late)

    own = lax.broadcasted_iota(jnp.int32, (2 * short, PAIR), 0)
    half = lax.broadcasted_iota(jnp.int32, (2 * short, PAIR), 1) // CH
    mask = ((place * columns + own) // CH % 2 == half) & (own < columns)
    entry = jnp.pad(memory.T, ((0, 2 * short - columns), (0, 0)))
    starts, final = call(
        scan_kernel,
        in_specs=[vmem, vmem, vmem, hbm],
        out_specs=[hbm, vmem],
        out_shape=[
            pltpu.HBM((owners, short, PAIR), F32),
            jax.ShapeDtypeStruct((2 * short, PAIR), F32),
        ],
        scratch_shapes=[pltpu.VMEM((owners, short, PAIR), F32), sems((owners // 4,))],
    )(slots, jnp.concatenate([entry, entry], axis=1), mask.astype(F32), base)
    starts = lax.all_to_all(starts, "ctx", 0, 0)
    exit_state = final[:columns, :CH].T

    out = call(
        functools.partial(final_kernel, columns=columns),
        in_specs=[vmem] * 5,
        out_specs=hbm,
        out_shape=pltpu.HBM((n, WIDTH), BF16),
        scratch_shapes=[pltpu.VMEM((WIDTH, PAIR), F32), tokens, sems((PAIRS,))],
    )(starts, read, local, base, gain.reshape(1, WIDTH))
    return out, exit_state


def solution(mesh):
    rows_spec = P(("dp", "ctx"), None)
    return jax.shard_map(
        shards,
        mesh=mesh,
        in_specs=(rows_spec,) * 6 + (P("dp", "ctx"), P(), P(), P()),
        out_specs=(rows_spec, P("dp", "ctx")),
        check_vma=False,
    )
```
